32 devices in a mesh: groups: 2 (over x), row: 16 (over z, y, core).
Axes of the slice: x: 2, y: 2, z: 4, core: 2. Of those that a mesh axis runs over, the one named last changes fastest.
Arguments:
- density_guess: bfloat16 [512, 128, 128], P(('groups', 'row')), parts along dimension 0, may hold values from -5 to 5
- cotangent: bfloat16 [512, 128, 128], P(('groups', 'row')), parts along dimension 0, may hold values from -6 to 6
- term_left: int32 [512, 4], P(('groups', 'row')), parts along dimension 0, may hold values from 0 to 15
- term_fetch: int32 [512, 4], P(('groups', 'row')), parts along dimension 0, may hold values from 0 to 31
- req_owner: int32 [1024, 1], P('groups'), parts along dimension 0, may hold values from 0 to 15; in each aligned block of 32 rows (0 to 31, 32 to 63, ...) at most 4 rows name the same one
- req_slot: int32 [1024], P('groups'), parts along dimension 0, may hold values from 0 to 15
Outputs:
- purified: bfloat16 [512, 128, 128], P(('groups', 'row')), parts along dimension 0
- guess_grad: float32 [512, 128, 128], P(('groups', 'row')), parts along dimension 0
The draws below stay inside these ranges and needn't reach their ends.
There are 2 independent parts, one for each index of `groups`. The reference program is written for one: setup_inputs(seed, part) draws one part's arguments, and reference() takes and returns one part's arrays. A program takes and returns all parts, laid end to end along the dimension named above; each array names one. Nothing has to cross between parts.
Inputs may be any that keep to these rules, and one draw needn't show every extreme that they name: `req_owner`: among the 32 requests of one group, at most 4 name the same owner; in every draw some group names some owner exactly 4 times.
All inputs are finite; a program needn't handle non-finite values.
Results may differ from the reference program's by a relative error of at most 0.009.
Values may be sent and summed in bfloat16 or wider, within the bound.
A program may use at most 128 MiB of HBM per device.

```python
import math
import jax
import jax.numpy as jnp
import numpy as np

BS = 128
TT = 4
REQ = 32
NB_DEV = 16
NB = 256
CAP = 4
N_ROW = 16


def plant(values, stream_key, least, largest):
    extent = values.shape
    index_at = [jax.random.randint(jax.random.fold_in(stream_key, axis), (), 0, extent[axis]) for axis in range(len(extent))]
    values = values.at[tuple(index_at)].set(least)
    longest = extent.index(max(extent))
    index_at[longest] = (index_at[longest] + 1) % extent[longest]
    return values.at[tuple(index_at)].set(largest)


def steps_of(stream_key, extent, split, least, top_value):
    def one(dim, parts):
        steps = jax.random.uniform(jax.random.fold_in(jax.random.fold_in(stream_key, 6), dim), (parts,), jnp.float32, least / len(split), top_value / len(split))
        return jnp.repeat(jnp.exp(steps), extent[dim] // parts).reshape((-1,) + (1,) * (len(extent) - dim - 1))

    loudness = one(*split[0])
    for cut in split[1:]:
        loudness = loudness * one(*cut)
    return loudness


def shared_out(key, own, number, rows, count, top, reach, slope):
    sequence = jax.random.permutation(key, count)
    heavy_load, common = portions_of(count, rows * top, reach, slope, True), portions_of(count, rows * top, reach, slope, False)
    places = jnp.arange(count)

    def named(lengths, offset_by):
        used = int((lengths > 0).sum())
        fixed = max(1, used // 4)
        moved = fixed + (places - fixed + offset_by * (used - fixed)) % max(1, count - fixed)
        return jnp.zeros((count,), jnp.int32).at[sequence[jnp.where(places < fixed, places, moved)]].set(jnp.asarray(lengths, jnp.int32))

    lengths = jnp.where(number % 4 == 0, named(heavy_load, number // 4), named(common, number - number // 4 - 1))
    mixed = jax.random.permutation(jax.random.fold_in(own, 3), count)
    source_of, taker = mixed[0:count // 2 * 2:2], mixed[1:count // 2 * 2:2]
    room = jnp.minimum(lengths[source_of] - 1, reach - lengths[taker]) // 2
    room = jnp.where((source_of == sequence[0]) | (taker == sequence[0]) | (lengths[taker] == 0), 0, jnp.maximum(room, 0))
    moved = jax.random.randint(jax.random.fold_in(own, 4), (count // 2,), 0, 1 << 20) % (room + 1)
    lengths = lengths.at[source_of].add(-moved).at[taker].add(moved)
    members = jnp.searchsorted(jnp.cumsum(lengths), jnp.arange(rows * top), side="right").astype(jnp.int32)
    listing = members.reshape(top, rows).T
    listing = listing[jax.random.permutation(jax.random.fold_in(own, 1), rows)]
    offset_by = jax.random.randint(jax.random.fold_in(own, 2), (rows, 1), 0, top)
    return jnp.take_along_axis(listing, (jnp.arange(top)[None, :] + offset_by) % top, axis=1)


def portions_of(amount, total, bound, lean, full):
    weights = [(1 << 20) // math.isqrt(standing ** lean) + 1 for standing in range(1, amount + 1)]
    largest = bound if full else min(bound, max(-(-total // amount), total * weights[0] // sum(weights)))
    least = 1 if total - largest >= amount - 1 else 0
    counts, surplus = [largest] + [least] * (amount - 1), total - largest - least * (amount - 1)
    while surplus > 0:
        candidates = [i for i in range(1, amount) if counts[i] < largest] or [i for i in range(1, amount) if counts[i] < bound]
        pool, budget = sum([weights[i] for i in candidates]), surplus
        for i in candidates:
            addition = min(bound - counts[i], max(1, budget * weights[i] // pool), surplus)
            counts[i] = counts[i] + addition
            surplus = surplus - addition
    return np.array(counts)


def centred(key, shape, spread, most, shards=(), held_as=jnp.bfloat16):
    array = jax.random.normal(key, shape, jnp.float32) * spread
    if len(shards) > 0:
        array = steps_of(key, shape, shards, -0.22, 0.18) * array
    return jnp.clip(array, min=-most, max=most).astype(held_as)


def setup_inputs(seed: int = 0, part: int = 0) -> dict:
    seeds = jax.random.split(jax.random.key(seed), 7)
    own_keys = jax.random.split(jax.random.fold_in(seeds[6], part), 7)
    density_guess = centred(own_keys[0], (NB, BS, BS), 0.8, 5.0, ((0, 16),))
    cotangent = centred(own_keys[1], (NB, BS, BS), 1.0, 6.0, ((0, 16),))
    term_left = plant(jax.random.randint(own_keys[2], (NB, TT), 0, NB_DEV), jax.random.fold_in(own_keys[2], 1), 0, NB_DEV - 1).astype(jnp.int32)
    term_fetch = plant(jax.random.randint(own_keys[3], (NB, TT), 0, REQ), jax.random.fold_in(own_keys[3], 1), 0, REQ - 1).astype(jnp.int32)
    req_owner_keys = jax.random.split(jax.random.fold_in(own_keys[4], 1), (N_ROW * REQ) // REQ)
    req_owner_turns = jax.random.permutation(jax.random.fold_in(own_keys[4], 3), (N_ROW * REQ) // REQ)
    req_owner = jax.vmap(lambda own, number: shared_out(jax.random.fold_in(own_keys[4], 2), own, number, REQ, N_ROW, 1, CAP, 2))(req_owner_keys, req_owner_turns).reshape((N_ROW * REQ, 1))
    req_slot = plant(jax.random.randint(own_keys[5], (N_ROW * REQ,), 0, NB_DEV), jax.random.fold_in(own_keys[5], 1), 0, NB_DEV - 1).astype(jnp.int32)
    return dict(density_guess=density_guess, cotangent=cotangent, term_left=term_left, term_fetch=term_fetch, req_owner=req_owner, req_slot=req_slot)


def block_tables(term_left, term_fetch, req_owner, req_slot):
    owner_of = jnp.arange(NB_DEV * N_ROW, dtype=jnp.int32) // NB_DEV
    left_global = owner_of[:, None] * NB_DEV + term_left
    request_global = owner_of[:, None] * REQ + term_fetch
    fetched_block = req_owner[:, 0] * NB_DEV + req_slot
    right_global = fetched_block[request_global]
    return left_global, right_global, request_global, fetched_block


def forward_product(left, right, tables, unit_scale):
    left_global, right_global = tables[0], tables[1]
    total = jnp.zeros(left.shape, jnp.float32)
    for column in range(TT):
        total = total + jnp.einsum('bik,bkj->bij', left[left_global[:, column]].astype(jnp.float32),
                                   right[right_global[:, column]].astype(jnp.float32))
    return unit_scale * total


def left_adjoint(cot, right, tables, unit_scale):
    left_global, right_global = tables[0], tables[1]
    total = jnp.zeros(cot.shape, jnp.float32)
    for column in range(TT):
        piece = jnp.einsum('bij,bkj->bik', cot.astype(jnp.float32), right[right_global[:, column]].astype(jnp.float32))
        total = total.at[left_global[:, column]].add(piece)
    return unit_scale * total


def request_adjoint(first, first_cot, second, second_cot, tables, unit_scale):
    left_global, request_global = tables[0], tables[2]
    total = jnp.zeros((N_ROW * REQ, BS, BS), jnp.float32)
    for column in range(TT):
        piece = jnp.einsum('bki,bkj->bij', first[left_global[:, column]].astype(jnp.float32), first_cot.astype(jnp.float32))
        piece = piece + jnp.einsum('bki,bkj->bij', second[left_global[:, column]].astype(jnp.float32), second_cot.astype(jnp.float32))
        total = total.at[request_global[:, column]].add(piece)
    return (unit_scale * total).astype(jnp.bfloat16)


def purify(density, tables, unit_scale):
    square = forward_product(density, density, tables, unit_scale).astype(jnp.bfloat16)
    cube = forward_product(square, density, tables, unit_scale)
    fresh = (3.0 * square.astype(jnp.float32) - 2.0 * cube).astype(jnp.bfloat16)
    return fresh, square


def reverse(density, square, cot, tables, unit_scale):
    cube_cot = (-2.0 * cot.astype(jnp.float32)).astype(jnp.bfloat16)
    square_cot = (3.0 * cot.astype(jnp.float32) + left_adjoint(cube_cot, density, tables, unit_scale)).astype(jnp.bfloat16)
    requests = request_adjoint(square, cube_cot, density, square_cot, tables, unit_scale)
    returned = jnp.zeros(density.shape, jnp.float32).at[tables[3]].add(requests.astype(jnp.float32))
    return left_adjoint(square_cot, density, tables, unit_scale) + returned


def reference(density_guess, cotangent, term_left, term_fetch, req_owner, req_slot):
    tables = block_tables(term_left, term_fetch, req_owner, req_slot)
    unit_scale = float(BS * TT) ** -0.5
    first, first_square = purify(density_guess, tables, unit_scale)
    second, second_square = purify(first, tables, unit_scale)
    first_cot = reverse(first, second_square, cotangent, tables, unit_scale).astype(jnp.bfloat16)
    guess_grad = reverse(density_guess, first_square, first_cot, tables, unit_scale)
    return second, guess_grad
```

```python
import functools

import jax
import jax.numpy as jnp
from jax import lax
from jax.experimental import pallas as pl
from jax.experimental.pallas import tpu as pltpu
from jax.sharding import PartitionSpec as P

F32 = jnp.float32
BF16 = jnp.bfloat16
VMEM_LIMIT = 56 * 1024 * 1024


def owner_tables(req_owner, req_slot, own_index, peer_count, slot_count, request_count):
    owners_all = req_owner[:, 0].reshape(peer_count, request_count)
    slots_all = req_slot.reshape(peer_count, request_count)
    mine = owners_all == own_index
    ranks = jnp.cumsum(mine.astype(jnp.int32), axis=1) - 1
    slot_ids = jnp.arange(slot_count, dtype=jnp.int32)
    chosen = mine[:, None, :] & (ranks[:, None, :] == slot_ids[None, :, None])
    send_index = jnp.sum(jnp.where(chosen, slots_all[:, None, :], 0), axis=2).reshape(-1)
    send_valid = jnp.any(chosen, axis=2).reshape(-1)
    own_owners = lax.dynamic_slice_in_dim(req_owner[:, 0], own_index * request_count, request_count)
    request_ids = jnp.arange(request_count, dtype=jnp.int32)
    earlier = (own_owners[:, None] == own_owners[None, :]) & (
        request_ids[None, :] < request_ids[:, None]
    )
    own_rank = jnp.sum(earlier.astype(jnp.int32), axis=1)
    receive_index = own_owners * slot_count + own_rank
    return (send_index, send_valid.astype(jnp.int32), receive_index)


def dot(a, b):
    return jnp.dot(a, b, preferred_element_type=F32)


def dot_rt(a, b):
    return lax.dot_general(a, b, (((1,), (1,)), ((), ())), preferred_element_type=F32)


def forward_sums(left, right, tl, tr, b, terms):
    lhs = jnp.concatenate([left[tl[b * terms + t]] for t in range(terms)], axis=1)
    rhs = jnp.concatenate([right[tr[b * terms + t]] for t in range(terms)], axis=0)
    return dot(lhs, rhs)


def left_adjoint(cots, right, tl, tr, acc, terms):
    acc[...] = jnp.zeros_like(acc)

    @pl.loop(0, cots.shape[0], unroll=2)
    def _(b):
        rhs = jnp.concatenate([right[tr[b * terms + t]] for t in range(terms)], axis=0)
        piece = dot_rt(cots[b], rhs)
        width = cots.shape[2]
        for t in range(terms):
            acc[tl[b * terms + t]] += piece[:, t * width:(t + 1) * width]


def gather_kernel(index, blocks, out):
    @pl.loop(0, out.shape[0], unroll=4)
    def _(s):
        out[s] = blocks[index[s]]


def forward_kernel(terms, scale, tl, tr, index, dens, right, fresh, square, *out):
    blocks = dens.shape[0]

    @pl.loop(0, blocks, unroll=4)
    def _(b):
        square[b] = (scale * forward_sums(dens, right, tl, tr, b, terms)).astype(BF16)

    @pl.loop(0, blocks, unroll=4)
    def _(b):
        cube = scale * forward_sums(square, right, tl, tr, b, terms)
        fresh[b] = (3.0 * square[b].astype(F32) - 2.0 * cube).astype(BF16)

    if out:
        gather_kernel(index, fresh, out[0])


def cot_phase(terms, scale, tl, tr, tf, rix, dens, square, right, cot, sqcot, sendback, acc, cube, both, racc):
    blocks, width = dens.shape[0], dens.shape[2]

    @pl.loop(0, blocks, unroll=4)
    def _(b):
        cube[b] = (-2.0 * cot[b].astype(F32)).astype(BF16)
        both[b] = jnp.concatenate([square[b].T, dens[b].T], axis=1)

    left_adjoint(cube, right, tl, tr, acc, terms)

    @pl.loop(0, blocks, unroll=4)
    def _(b):
        sqcot[b] = (3.0 * cot[b].astype(F32) + scale * acc[b]).astype(BF16)

    racc[...] = jnp.zeros_like(racc)

    @pl.loop(0, blocks, unroll=2)
    def _(b):
        lhs = jnp.concatenate([both[tl[b * terms + t]] for t in range(terms)], axis=0)
        rhs = jnp.concatenate([cube[b], sqcot[b]], axis=0)
        piece = dot(lhs, rhs)
        for t in range(terms):
            racc[tf[b * terms + t]] += piece[t * width:(t + 1) * width]

    @pl.loop(0, sendback.shape[0], unroll=4)
    def _(s):
        sendback[s] = jnp.zeros(sendback.shape[1:], BF16)

    @pl.loop(0, racc.shape[0], unroll=4)
    def _(q):
        sendback[rix[q]] = (scale * racc[q]).astype(BF16)


def reverse_kernel(terms, scale, tl, tr, tf, rix, dens, square, right, cot, sqcot, sendback, acc, cube, both, racc):
    cot_phase(terms, scale, tl, tr, tf, rix, dens, square, right, cot, sqcot, sendback, acc, cube, both, racc)


def collect(index, valid, returned, grad):
    @pl.loop(0, returned.shape[0])
    def _(s):
        @pl.when(valid[s] > 0)
        def _():
            grad[index[s]] += returned[s].astype(F32)


def chained_kernel(terms, scale, tl, tr, tf, rix, index, valid, dens, square, right, local, returned, sqcot, sendback, acc, cube, both, racc, cot):
    acc[...] = local[...]
    collect(index, valid, returned, acc)
    cot[...] = acc[...].astype(BF16)
    cot_phase(terms, scale, tl, tr, tf, rix, dens, square, right, cot, sqcot, sendback, acc, cube, both, racc)


def local_kernel(terms, scale, tl, tr, sqcot, right, grad):
    left_adjoint(sqcot, right, tl, tr, grad, terms)
    grad[...] = scale * grad[...]


def final_kernel(index, valid, local, returned, grad):
    grad[...] = local[...]
    collect(index, valid, returned, grad)


def call(kernel, prefetch, arrays, outs, scratch=(), flops=0):
    whole = pl.BlockSpec(memory_space=pltpu.VMEM)
    smem = pl.BlockSpec(memory_space=pltpu.SMEM)
    moved = sum(a.size * a.dtype.itemsize for a in arrays)
    return pl.pallas_call(
        kernel,
        out_shape=outs,
        in_specs=[smem] * len(prefetch) + [whole] * len(arrays),
        out_specs=[whole] * len(outs),
        scratch_shapes=list(scratch),
        cost_estimate=pl.CostEstimate(flops=flops, bytes_accessed=moved, transcendentals=0),
        compiler_params=pltpu.CompilerParams(vmem_limit_bytes=VMEM_LIMIT),
    )(*prefetch, *arrays)


def body(density_guess, cotangent, term_left, term_fetch, req_owner, req_slot):
    peer_count = lax.axis_size("row")
    own_index = lax.axis_index("row")
    request_count = req_owner.shape[0] // peer_count
    slot_count = max(2, 2 * request_count // peer_count)
    blocks, width = density_guess.shape[0], density_guess.shape[1]
    terms = term_left.shape[1]
    scale = float(width * terms) ** (-0.5)
    send_index, send_valid, receive_index = owner_tables(
        req_owner, req_slot, own_index, peer_count, slot_count, request_count
    )
    slots = peer_count * slot_count
    tl = term_left.reshape(-1)
    tf = term_fetch.reshape(-1)
    tr = receive_index[tf]

    def shape(n, dtype):
        return jax.ShapeDtypeStruct((n, width, width), dtype)

    def exchange(x):
        return lax.all_to_all(x, "row", split_axis=0, concat_axis=0, tiled=True)

    work = 2 * blocks * terms * width ** 3
    common = [
        pltpu.VMEM((blocks, width, width), F32),
        pltpu.VMEM((blocks, width, width), BF16),
        pltpu.VMEM((blocks, width, 2 * width), BF16),
        pltpu.VMEM((request_count, width, width), F32),
    ]
    forward = functools.partial(forward_kernel, terms, scale)
    (out0,) = call(gather_kernel, [send_index], [density_guess], [shape(slots, BF16)])
    right0 = exchange(out0)
    first, square1, out1 = call(
        forward, [tl, tr, send_index], [density_guess, right0],
        [shape(blocks, BF16), shape(blocks, BF16), shape(slots, BF16)], flops=2 * work)
    right1 = exchange(out1)
    second, square2 = call(
        forward, [tl, tr, send_index], [first, right1],
        [shape(blocks, BF16), shape(blocks, BF16)], flops=2 * work)
    sqcot2, back2 = call(
        functools.partial(reverse_kernel, terms, scale), [tl, tr, tf, receive_index],
        [first, square2, right1, cotangent],
        [shape(blocks, BF16), shape(slots, BF16)], common, flops=3 * work)
    returned2 = exchange(back2)
    local = functools.partial(local_kernel, terms, scale)
    (local2,) = call(local, [tl, tr], [sqcot2, right1], [shape(blocks, F32)], flops=work)
    sqcot1, back1 = call(
        functools.partial(chained_kernel, terms, scale),
        [tl, tr, tf, receive_index, send_index, send_valid],
        [density_guess, square1, right0, local2, returned2],
        [shape(blocks, BF16), shape(slots, BF16)],
        common + [pltpu.VMEM((blocks, width, width), BF16)], flops=3 * work)
    returned1 = exchange(back1)
    (local1,) = call(local, [tl, tr], [sqcot1, right0], [shape(blocks, F32)], flops=work)
    (grad,) = call(final_kernel, [send_index, send_valid], [local1, returned1], [shape(blocks, F32)])
    return (second, grad)


def solution(mesh):
    placed = (
        P(("groups", "row"), None, None),
        P(("groups", "row"), None, None),
        P(("groups", "row"), None),
        P(("groups", "row"), None),
        P("groups", None),
        P("groups"),
    )
    return jax.shard_map(
        body,
        mesh=mesh,
        in_specs=placed,
        out_specs=(P(("groups", "row"), None, None), P(("groups", "row"), None, None)),
        check_vma=False,
    )
```

```python
import functools

import jax
import jax.numpy as jnp
from jax import lax
from jax.experimental import pallas as pl
from jax.experimental.pallas import tpu as pltpu
from jax.sharding import PartitionSpec as P

F32 = jnp.float32
BF16 = jnp.bfloat16
VMEM_LIMIT = 56 * 1024 * 1024
GATHER_BYTES = 16 * 1024 * 1024


def owner_tables(req_owner, req_slot, own_index, peer_count, slot_count, request_count):
    owners_all = req_owner[:, 0].reshape(peer_count, request_count)
    slots_all = req_slot.reshape(peer_count, request_count)
    mine = owners_all == own_index
    ranks = jnp.cumsum(mine.astype(jnp.int32), axis=1) - 1
    slot_ids = jnp.arange(slot_count, dtype=jnp.int32)
    chosen = mine[:, None, :] & (ranks[:, None, :] == slot_ids[None, :, None])
    send_index = jnp.sum(jnp.where(chosen, slots_all[:, None, :], 0), axis=2).reshape(-1)
    send_valid = jnp.any(chosen, axis=2).reshape(-1)
    own_owners = lax.dynamic_slice_in_dim(req_owner[:, 0], own_index * request_count, request_count)
    request_ids = jnp.arange(request_count, dtype=jnp.int32)
    earlier = (own_owners[:, None] == own_owners[None, :]) & (
        request_ids[None, :] < request_ids[:, None]
    )
    own_rank = jnp.sum(earlier.astype(jnp.int32), axis=1)
    receive_index = own_owners * slot_count + own_rank
    return (send_index, send_valid.astype(jnp.int32), receive_index)


def dot(a, b):
    return jnp.dot(a, b, preferred_element_type=F32)


def dot_rt(a, b):
    return lax.dot_general(a, b, (((1,), (1,)), ((), ())), preferred_element_type=F32)


def forward_sums(left, right, tl, tr, b, terms):
    lhs = jnp.concatenate([left[tl[b * terms + t]] for t in range(terms)], axis=1)
    rhs = jnp.concatenate([right[tr[b * terms + t]] for t in range(terms)], axis=0)
    return dot(lhs, rhs)


def left_adjoint(cots, right, tl, tr, acc, terms):
    acc[...] = jnp.zeros_like(acc)

    @pl.loop(0, cots.shape[0], unroll=2)
    def _(b):
        rhs = jnp.concatenate([right[tr[b * terms + t]] for t in range(terms)], axis=0)
        piece = dot_rt(cots[b], rhs)
        width = cots.shape[2]
        for t in range(terms):
            acc[tl[b * terms + t]] += piece[:, t * width:(t + 1) * width]


def gather_kernel(index, blocks, out):
    @pl.loop(0, out.shape[0], unroll=4)
    def _(s):
        out[s] = blocks[index[s]]


def forward_kernel(terms, scale, tl, tr, index, dens, right, fresh, square, *out):
    blocks = dens.shape[0]

    @pl.loop(0, blocks, unroll=4)
    def _(b):
        square[b] = (scale * forward_sums(dens, right, tl, tr, b, terms)).astype(BF16)

    @pl.loop(0, blocks, unroll=4)
    def _(b):
        cube = scale * forward_sums(square, right, tl, tr, b, terms)
        fresh[b] = (3.0 * square[b].astype(F32) - 2.0 * cube).astype(BF16)

    if out:
        gather_kernel(index, fresh, out[0])


def cot_phase(terms, scale, tl, tr, tf, rix, dens, square, right, cot, sqcot, sendback, acc, cube, both, racc):
    blocks, width = dens.shape[0], dens.shape[2]

    @pl.loop(0, blocks, unroll=4)
    def _(b):
        cube[b] = (-2.0 * cot[b].astype(F32)).astype(BF16)
        both[b] = jnp.concatenate([square[b].T, dens[b].T], axis=1)

    left_adjoint(cube, right, tl, tr, acc, terms)

    @pl.loop(0, blocks, unroll=4)
    def _(b):
        sqcot[b] = (3.0 * cot[b].astype(F32) + scale * acc[b]).astype(BF16)

    racc[...] = jnp.zeros_like(racc)

    @pl.loop(0, blocks, unroll=2)
    def _(b):
        lhs = jnp.concatenate([both[tl[b * terms + t]] for t in range(terms)], axis=0)
        rhs = jnp.concatenate([cube[b], sqcot[b]], axis=0)
        piece = dot(lhs, rhs)
        for t in range(terms):
            racc[tf[b * terms + t]] += piece[t * width:(t + 1) * width]

    @pl.loop(0, sendback.shape[0], unroll=4)
    def _(s):
        sendback[s] = jnp.zeros(sendback.shape[1:], BF16)

    @pl.loop(0, racc.shape[0], unroll=4)
    def _(q):
        sendback[rix[q]] = (scale * racc[q]).astype(BF16)


def reverse_kernel(terms, scale, tl, tr, tf, rix, dens, square, right, cot, sqcot, sendback, acc, cube, both, racc):
    cot_phase(terms, scale, tl, tr, tf, rix, dens, square, right, cot, sqcot, sendback, acc, cube, both, racc)


def collect(index, valid, returned, grad):
    @pl.loop(0, returned.shape[0])
    def _(s):
        @pl.when(valid[s] > 0)
        def _():
            grad[index[s]] += returned[s].astype(F32)


def chained_kernel(terms, scale, tl, tr, tf, rix, index, valid, dens, square, right, local, returned, sqcot, sendback, acc, cube, both, racc, cot):
    acc[...] = local[...]
    collect(index, valid, returned, acc)
    cot[...] = acc[...].astype(BF16)
    cot_phase(terms, scale, tl, tr, tf, rix, dens, square, right, cot, sqcot, sendback, acc, cube, both, racc)


def local_kernel(terms, scale, tl, tr, sqcot, right, grad):
    left_adjoint(sqcot, right, tl, tr, grad, terms)
    grad[...] = scale * grad[...]


def final_kernel(index, valid, local, returned, grad):
    grad[...] = local[...]
    collect(index, valid, returned, grad)


def spread_kernel(nz, ny, nc, parts, own, spread, send_sem, recv_sem, own_sem):
    me = lax.axis_index("row")
    core, y, z = me % nc, (me // nc) % ny, me // (nc * ny)
    count = own.shape[0]
    size = count // parts
    UP, DOWN, ACROSS, TWIN = 0, 1, 2, 3
    steps = {UP: nc * ny, DOWN: -nc * ny}

    def target(way):
        if way == ACROSS:
            return (z * ny + (ny - 1 - y)) * nc + core
        if way == TWIN:
            return (z * ny + y) * nc + (nc - 1 - core)
        return me + steps[way]

    def exists(way):
        return {UP: z + 1 < nz, DOWN: z > 0}[way]

    barrier = pltpu.get_barrier_semaphore()

    def greet(way):
        pl.semaphore_signal(barrier, inc=1, device_id={"row": target(way)}, device_id_type=pl.DeviceIdType.MESH)

    for way in (UP, DOWN):
        pl.when(exists(way))(functools.partial(greet, way))
    for way in (ACROSS, TWIN):
        greet(way)
    pl.semaphore_wait(barrier, 2 + (z + 1 < nz).astype(jnp.int32) + (z > 0).astype(jnp.int32))

    def copy(way, zz, yy, s, from_own=False):
        origin = (zz * ny + yy) * nc + core
        place = spread.at[pl.ds(origin * count + s * size, size)]
        source = own.at[pl.ds(s * size, size)] if from_own else place
        return pltpu.make_async_remote_copy(
            src_ref=source, dst_ref=place,
            send_sem=send_sem.at[way, zz * ny + yy, s], recv_sem=recv_sem.at[origin, s],
            device_id={"row": target(way)}, device_id_type=pl.DeviceIdType.MESH)

    def arrived(zz, yy, s, plane):
        origin = (zz * ny + yy) * nc + plane
        place = spread.at[pl.ds(origin * count + s * size, size)]
        pltpu.make_async_remote_copy(
            src_ref=place, dst_ref=place,
            send_sem=send_sem.at[TWIN, 0, 0], recv_sem=recv_sem.at[origin, s],
            device_id={"row": target(TWIN)}, device_id_type=pl.DeviceIdType.MESH).wait_recv()

    def maybe(way, act):
        pl.when(exists(way))(act)

    kept = pltpu.make_async_copy(own, spread.at[pl.ds(me * count, count)], own_sem)
    kept.start()

    @pl.loop(0, parts)
    def _(s):
        maybe(UP, lambda: copy(UP, z, y, s, True).start())
        maybe(DOWN, lambda: copy(DOWN, z, y, s, True).start())
        copy(ACROSS, z, y, s, True).start()
        copy(TWIN, z, y, s, True).start()

    def along(d, s, yy, cross):
        for way, zz, there in ((UP, z - d, z >= d), (DOWN, z + d, z + d < nz)):
            @pl.when(there)
            def _(way=way, zz=zz):
                arrived(zz, yy, s, core)
                maybe(way, lambda: copy(way, zz, yy, s).start())
                if cross:
                    copy(ACROSS, zz, yy, s).start()
                copy(TWIN, zz, yy, s).start()

    other = ny - 1 - y
    arrived(z, other, 0, core)
    maybe(UP, lambda: copy(UP, z, other, 0).start())
    maybe(DOWN, lambda: copy(DOWN, z, other, 0).start())
    copy(TWIN, z, other, 0).start()

    def crossed(d, s):
        if d == 0:
            arrived(z, other, s, core)
            copy(TWIN, z, other, s).start()
        else:
            for zz, there in ((z - d, z >= d), (z + d, z + d < nz)):
                @pl.when(there)
                def _(zz=zz):
                    arrived(zz, other, s, core)
                    copy(TWIN, zz, other, s).start()

    for d in range(1, nz):
        along(d, 0, y, False)

        @pl.loop(1, parts)
        def _(s):
            along(d, s, y, True)
            crossed(d - 1, s)

        along(d, 0, other, False)

    @pl.loop(1, parts)
    def _(s):
        crossed(nz - 1, s)

    kept.wait()

    @pl.loop(0, nz * ny * parts)
    def _(i):
        arrived(i // (ny * parts), (i // parts) % ny, i % parts, nc - 1 - core)

    def sent(way, zz, yy, s):
        copy(way, zz, yy, s).wait_send()

    @pl.loop(0, nz * parts)
    def _(i):
        zz, s = i // parts, i % parts
        for yy in range(ny):
            sent(TWIN, zz, yy, s)

        @pl.when((s > 0) | (zz == z))
        def _():
            sent(ACROSS, zz, y, s)

        @pl.when((zz <= z) & (z + 1 < nz))
        def _():
            sent(UP, zz, y, s)

        @pl.when((zz >= z) & (z > 0))
        def _():
            sent(DOWN, zz, y, s)

        @pl.when((s == 0) & (zz <= z) & (z + 1 < nz))
        def _():
            sent(UP, zz, other, s)

        @pl.when((s == 0) & (zz >= z) & (z > 0))
        def _():
            sent(DOWN, zz, other, s)


def spread_all(own, peers):
    nc, ny = 2, 2
    nz, parts = peers // (nc * ny), 8
    count, width = own.shape[0], own.shape[1]
    return pl.pallas_call(
        functools.partial(spread_kernel, nz, ny, nc, parts),
        out_shape=jax.ShapeDtypeStruct((peers * count, width, width), own.dtype),
        in_specs=[pl.BlockSpec(memory_space=pl.ANY)],
        out_specs=pl.BlockSpec(memory_space=pl.ANY),
        scratch_shapes=[
            pltpu.SemaphoreType.DMA((4, nz * ny, parts)),
            pltpu.SemaphoreType.DMA((peers, parts)),
            pltpu.SemaphoreType.DMA,
        ],
        compiler_params=pltpu.CompilerParams(collective_id=0, has_side_effects=True),
    )(own)


def rebuild_kernel(terms, scale, count, requests, first_block, first_request, tl, tf, blk, whole, fresh, square, right0, right1, squares):
    total = whole.shape[0]

    def term_ids(b):
        group = b // count
        lefts = [group * count + tl[b * terms + t] for t in range(terms)]
        rights = [blk[group * requests + tf[b * terms + t]] for t in range(terms)]
        return lefts, rights

    def product(left, b):
        lefts, rights = term_ids(b)
        lhs = jnp.concatenate([left[i] for i in lefts], axis=1)
        rhs = jnp.concatenate([whole[i] for i in rights], axis=0)
        return scale * dot(lhs, rhs)

    @pl.loop(0, total, unroll=8)
    def _(b):
        squares[b] = product(whole, b).astype(BF16)

    def purified(b):
        return (3.0 * squares[b].astype(F32) - 2.0 * product(squares, b)).astype(BF16)

    start = first_block[0]

    @pl.loop(0, count, unroll=8)
    def _(b):
        square[b] = squares[start + b]
        fresh[b] = purified(start + b)

    start_request = first_request[0]

    @pl.loop(0, requests, unroll=8)
    def _(q):
        b = blk[start_request + q]
        right0[q] = whole[b]
        right1[q] = purified(b)


def call(kernel, prefetch, arrays, outs, scratch=(), flops=0):
    whole = pl.BlockSpec(memory_space=pltpu.VMEM)
    smem = pl.BlockSpec(memory_space=pltpu.SMEM)
    moved = sum(a.size * a.dtype.itemsize for a in arrays)
    return pl.pallas_call(
        kernel,
        out_shape=outs,
        in_specs=[smem] * len(prefetch) + [whole] * len(arrays),
        out_specs=[whole] * len(outs),
        scratch_shapes=list(scratch),
        cost_estimate=pl.CostEstimate(flops=flops, bytes_accessed=moved, transcendentals=0),
        compiler_params=pltpu.CompilerParams(vmem_limit_bytes=VMEM_LIMIT),
    )(*prefetch, *arrays)


def body(density_guess, cotangent, term_left, term_fetch, req_owner, req_slot):
    peer_count = lax.axis_size("row")
    own_index = lax.axis_index("row")
    request_count = req_owner.shape[0] // peer_count
    slot_count = max(2, 2 * request_count // peer_count)
    blocks, width = density_guess.shape[0], density_guess.shape[1]
    terms = term_left.shape[1]
    scale = float(width * terms) ** (-0.5)
    send_index, send_valid, receive_index = owner_tables(
        req_owner, req_slot, own_index, peer_count, slot_count, request_count
    )
    slots = peer_count * slot_count
    tl = term_left.reshape(-1)
    tf = term_fetch.reshape(-1)

    def shape(n, dtype):
        return jax.ShapeDtypeStruct((n, width, width), dtype)

    def exchange(x):
        return lax.all_to_all(x, "row", split_axis=0, concat_axis=0, tiled=True)

    work = 2 * blocks * terms * width ** 3
    common = [
        pltpu.VMEM((blocks, width, width), F32),
        pltpu.VMEM((blocks, width, width), BF16),
        pltpu.VMEM((blocks, width, 2 * width), BF16),
        pltpu.VMEM((request_count, width, width), F32),
    ]
    forward = functools.partial(forward_kernel, terms, scale)
    if peer_count * blocks * width * width * 2 <= GATHER_BYTES and peer_count % 4 == 0:
        tables = lax.all_gather(jnp.concatenate([term_left, term_fetch], axis=1), "row", tiled=True)
        all_left = tables[:, :terms].reshape(-1)
        all_fetch = tables[:, terms:].reshape(-1)
        named = req_owner[:, 0] * blocks + req_slot
        whole = spread_all(density_guess, peer_count)
        first, square1, right0, right1 = call(
            functools.partial(rebuild_kernel, terms, scale, blocks, request_count),
            [(own_index * blocks).reshape(1), (own_index * request_count).reshape(1), all_left, all_fetch, named], [whole],
            [shape(blocks, BF16), shape(blocks, BF16), shape(request_count, BF16), shape(request_count, BF16)],
            [pltpu.VMEM((peer_count * blocks, width, width), BF16)], flops=(peer_count + 3) * work)
        tr = tf
    else:
        tr = receive_index[tf]
        (out0,) = call(gather_kernel, [send_index], [density_guess], [shape(slots, BF16)])
        right0 = exchange(out0)
        first, square1, out1 = call(
            forward, [tl, tr, send_index], [density_guess, right0],
            [shape(blocks, BF16), shape(blocks, BF16), shape(slots, BF16)], flops=2 * work)
        right1 = exchange(out1)
    second, square2 = call(
        forward, [tl, tr, send_index], [first, right1],
        [shape(blocks, BF16), shape(blocks, BF16)], flops=2 * work)
    sqcot2, back2 = call(
        functools.partial(reverse_kernel, terms, scale), [tl, tr, tf, receive_index],
        [first, square2, right1, cotangent],
        [shape(blocks, BF16), shape(slots, BF16)], common, flops=3 * work)
    returned2 = exchange(back2)
    local = functools.partial(local_kernel, terms, scale)
    (local2,) = call(local, [tl, tr], [sqcot2, right1], [shape(blocks, F32)], flops=work)
    sqcot1, back1 = call(
        functools.partial(chained_kernel, terms, scale),
        [tl, tr, tf, receive_index, send_index, send_valid],
        [density_guess, square1, right0, local2, returned2],
        [shape(blocks, BF16), shape(slots, BF16)],
        common + [pltpu.VMEM((blocks, width, width), BF16)], flops=3 * work)
    returned1 = exchange(back1)
    (local1,) = call(local, [tl, tr], [sqcot1, right0], [shape(blocks, F32)], flops=work)
    (grad,) = call(final_kernel, [send_index, send_valid], [local1, returned1], [shape(blocks, F32)])
    return (second, grad)


def solution(mesh):
    placed = (
        P(("groups", "row"), None, None),
        P(("groups", "row"), None, None),
        P(("groups", "row"), None),
        P(("groups", "row"), None),
        P("groups", None),
        P("groups"),
    )
    return jax.shard_map(
        body,
        mesh=mesh,
        in_specs=placed,
        out_specs=(P(("groups", "row"), None, None), P(("groups", "row"), None, None)),
        check_vma=False,
    )
```

```python
import functools

import jax
import jax.numpy as jnp
from jax import lax
from jax.experimental import pallas as pl
from jax.experimental.pallas import tpu as pltpu
from jax.sharding import PartitionSpec as P

F32 = jnp.float32
BF16 = jnp.bfloat16
VMEM_LIMIT = 56 * 1024 * 1024
GATHER_BYTES = 16 * 1024 * 1024


def owner_tables(req_owner, req_slot, own_index, peer_count, slot_count, request_count):
    owners_all = req_owner[:, 0].reshape(peer_count, request_count)
    slots_all = req_slot.reshape(peer_count, request_count)
    mine = owners_all == own_index
    ranks = jnp.cumsum(mine.astype(jnp.int32), axis=1) - 1
    slot_ids = jnp.arange(slot_count, dtype=jnp.int32)
    chosen = mine[:, None, :] & (ranks[:, None, :] == slot_ids[None, :, None])
    send_index = jnp.sum(jnp.where(chosen, slots_all[:, None, :], 0), axis=2).reshape(-1)
    own_owners = lax.dynamic_slice_in_dim(req_owner[:, 0], own_index * request_count, request_count)
    request_ids = jnp.arange(request_count, dtype=jnp.int32)
    earlier = (own_owners[:, None] == own_owners[None, :]) & (
        request_ids[None, :] < request_ids[:, None]
    )
    own_rank = jnp.sum(earlier.astype(jnp.int32), axis=1)
    receive_index = own_owners * slot_count + own_rank
    return (send_index, receive_index)


def dot(a, b):
    return jnp.dot(a, b, preferred_element_type=F32)


def dot_rt(a, b):
    return lax.dot_general(a, b, (((1,), (1,)), ((), ())), preferred_element_type=F32)


def forward_sums(left, right, tl, tr, b, terms):
    lhs = jnp.concatenate([left[tl[b, t]] for t in range(terms)], axis=1)
    rhs = jnp.concatenate([right[tr[b, t]] for t in range(terms)], axis=0)
    return dot(lhs, rhs)


def left_adjoint(cots, right, tl, tr, acc, terms):
    acc[...] = jnp.zeros_like(acc)

    @pl.loop(0, cots.shape[0], unroll=8)
    def _(b):
        rhs = jnp.concatenate([right[tr[b, t]] for t in range(terms)], axis=0)
        piece = dot_rt(cots[b], rhs)
        width = cots.shape[2]
        for t in range(terms):
            acc[tl[b, t]] += piece[:, t * width:(t + 1) * width]


def gather_kernel(index, blocks, out):
    @pl.loop(0, out.shape[0], unroll=4)
    def _(s):
        out[s] = blocks[index[s]]


def square_phase(terms, scale, tl, tr, dens, right, square):
    @pl.loop(0, dens.shape[0], unroll=16)
    def _(b):
        square[b] = (scale * forward_sums(dens, right, tl, tr, b, terms)).astype(BF16)


def fresh_phase(terms, scale, tl, tr, square, right, fresh):
    @pl.loop(0, square.shape[0], unroll=16)
    def _(b):
        cube = scale * forward_sums(square, right, tl, tr, b, terms)
        fresh[b] = (3.0 * square[b].astype(F32) - 2.0 * cube).astype(BF16)


def forward_kernel(terms, scale, tl, tr, index, dens, right, fresh, square, out):
    square_phase(terms, scale, tl, tr, dens, right, square)
    fresh_phase(terms, scale, tl, tr, square, right, fresh)
    gather_kernel(index, fresh, out)


def cot_phase(terms, scale, tl, tr, tf, rix, dens, square, right, cot, sqcot, sendback, acc, cube, both, racc):
    blocks, width = dens.shape[0], dens.shape[2]

    @pl.loop(0, blocks, unroll=4)
    def _(b):
        cube[b] = (-2.0 * cot[b].astype(F32)).astype(BF16)
        both[b] = jnp.concatenate([square[b].T, dens[b].T], axis=1)

    left_adjoint(cube, right, tl, tr, acc, terms)

    @pl.loop(0, blocks, unroll=4)
    def _(b):
        sqcot[b] = (3.0 * cot[b].astype(F32) + scale * acc[b]).astype(BF16)

    racc[...] = jnp.zeros_like(racc)

    @pl.loop(0, blocks, unroll=8)
    def _(b):
        lhs = jnp.concatenate([both[tl[b, t]] for t in range(terms)], axis=0)
        rhs = jnp.concatenate([cube[b], sqcot[b]], axis=0)
        piece = dot(lhs, rhs)
        for t in range(terms):
            racc[tf[b, t]] += piece[t * width:(t + 1) * width]

    @pl.loop(0, sendback.shape[0], unroll=4)
    def _(s):
        sendback[s] = jnp.zeros(sendback.shape[1:], BF16)

    @pl.loop(0, racc.shape[0], unroll=4)
    def _(q):
        sendback[rix[q]] = (scale * racc[q]).astype(BF16)


def reverse_kernel(terms, scale, tl, tr, tf, rix, dens, right, cot, square, sqcot, sendback, acc, cube, both, racc):
    square_phase(terms, scale, tl, tr, dens, right, square)
    cot_phase(terms, scale, tl, tr, tf, rix, dens, square, right, cot, sqcot, sendback, acc, cube, both, racc)


def collect(index, returned, grad):
    @pl.loop(0, returned.shape[0], unroll=8)
    def _(s):
        grad[index[s]] += returned[s].astype(F32)


def chained_kernel(terms, scale, tl, tr, tf, rix, index, dens, square, right, local, returned, sqcot, sendback, acc, cube, both, racc, cot):
    acc[...] = local[...]
    collect(index, returned, acc)
    cot[...] = acc[...].astype(BF16)
    cot_phase(terms, scale, tl, tr, tf, rix, dens, square, right, cot, sqcot, sendback, acc, cube, both, racc)


def local_kernel(terms, scale, tl, tr, sqcot, right, grad):
    left_adjoint(sqcot, right, tl, tr, grad, terms)
    grad[...] = scale * grad[...]


def final_kernel(index, local, returned, grad):
    grad[...] = local[...]
    collect(index, returned, grad)


def spread_kernel(nz, ny, nc, parts, own, own_tab, spread, tabs, send_sem, recv_sem, own_sem):
    me = lax.axis_index("row")
    core, y, z = me % nc, (me // nc) % ny, me // (nc * ny)
    count = own.shape[0]
    size = count // parts
    UP, DOWN, ACROSS, TWIN = 0, 1, 2, 3
    steps = {UP: nc * ny, DOWN: -nc * ny}

    def target(way):
        if way == ACROSS:
            return (z * ny + (ny - 1 - y)) * nc + core
        if way == TWIN:
            return (z * ny + y) * nc + (nc - 1 - core)
        return me + steps[way]

    def exists(way):
        return {UP: z + 1 < nz, DOWN: z > 0}[way]

    barrier = pltpu.get_barrier_semaphore()

    def greet(way):
        pl.semaphore_signal(barrier, inc=1, device_id={"row": target(way)}, device_id_type=pl.DeviceIdType.MESH)

    for way in (UP, DOWN):
        pl.when(exists(way))(functools.partial(greet, way))
    for way in (ACROSS, TWIN):
        greet(way)
    pl.semaphore_wait(barrier, 2 + (z + 1 < nz).astype(jnp.int32) + (z > 0).astype(jnp.int32))

    TAB = parts

    def place_of(origin, s):
        if s is TAB:
            return tabs.at[origin]
        return spread.at[pl.ds(origin * count + s * size, size)]

    def copy(way, zz, yy, s, from_own=False):
        origin = (zz * ny + yy) * nc + core
        place = source = place_of(origin, s)
        if from_own:
            source = own_tab if s is TAB else own.at[pl.ds(s * size, size)]
        return pltpu.make_async_remote_copy(
            src_ref=source, dst_ref=place,
            send_sem=send_sem.at[way, zz * ny + yy, s], recv_sem=recv_sem.at[origin, s],
            device_id={"row": target(way)}, device_id_type=pl.DeviceIdType.MESH)

    def arrived(zz, yy, s, plane):
        origin = (zz * ny + yy) * nc + plane
        place = place_of(origin, s)
        pltpu.make_async_remote_copy(
            src_ref=place, dst_ref=place,
            send_sem=send_sem.at[TWIN, 0, 0], recv_sem=recv_sem.at[origin, s],
            device_id={"row": target(TWIN)}, device_id_type=pl.DeviceIdType.MESH).wait_recv()

    def maybe(way, act):
        pl.when(exists(way))(act)

    kept = pltpu.make_async_copy(own, spread.at[pl.ds(me * count, count)], own_sem.at[0])
    kept.start()
    kept_tab = pltpu.make_async_copy(own_tab, tabs.at[me], own_sem.at[1])
    kept_tab.start()

    def begin(s):
        maybe(UP, lambda: copy(UP, z, y, s, True).start())
        maybe(DOWN, lambda: copy(DOWN, z, y, s, True).start())
        copy(ACROSS, z, y, s, True).start()
        copy(TWIN, z, y, s, True).start()

    begin(TAB)
    pl.loop(0, parts)(begin)

    def along(d, s, yy, cross):
        for way, zz, there in ((UP, z - d, z >= d), (DOWN, z + d, z + d < nz)):
            @pl.when(there)
            def _(way=way, zz=zz):
                arrived(zz, yy, s, core)
                maybe(way, lambda: copy(way, zz, yy, s).start())
                if cross:
                    copy(ACROSS, zz, yy, s).start()
                copy(TWIN, zz, yy, s).start()

    other = ny - 1 - y
    arrived(z, other, 0, core)
    maybe(UP, lambda: copy(UP, z, other, 0).start())
    maybe(DOWN, lambda: copy(DOWN, z, other, 0).start())
    copy(TWIN, z, other, 0).start()

    def crossed(d, s):
        if d == 0:
            arrived(z, other, s, core)
            copy(TWIN, z, other, s).start()
        else:
            for zz, there in ((z - d, z >= d), (z + d, z + d < nz)):
                @pl.when(there)
                def _(zz=zz):
                    arrived(zz, other, s, core)
                    copy(TWIN, zz, other, s).start()

    for d in range(1, nz):
        along(d, 0, y, False)
        along(d, TAB, y, True)
        crossed(d - 1, TAB)

        @pl.loop(1, parts)
        def _(s):
            along(d, s, y, True)
            crossed(d - 1, s)

        along(d, 0, other, False)

    crossed(nz - 1, TAB)

    @pl.loop(1, parts)
    def _(s):
        crossed(nz - 1, s)

    kept.wait()
    kept_tab.wait()

    @pl.loop(0, nz * ny)
    def _(i):
        arrived(i // ny, i % ny, TAB, nc - 1 - core)

        @pl.loop(0, parts)
        def _(s):
            arrived(i // ny, i % ny, s, nc - 1 - core)

    def sent(way, zz, yy, s):
        copy(way, zz, yy, s).wait_send()

    def finish(zz, s, first):
        for yy in range(ny):
            sent(TWIN, zz, yy, s)

        @pl.when(jnp.logical_or(jnp.logical_not(first), zz == z))
        def _():
            sent(ACROSS, zz, y, s)

        @pl.when((zz <= z) & (z + 1 < nz))
        def _():
            sent(UP, zz, y, s)

        @pl.when((zz >= z) & (z > 0))
        def _():
            sent(DOWN, zz, y, s)

        if s is not TAB:
            @pl.when(first & (zz <= z) & (z + 1 < nz))
            def _():
                sent(UP, zz, other, s)

            @pl.when(first & (zz >= z) & (z > 0))
            def _():
                sent(DOWN, zz, other, s)

    @pl.loop(0, nz)
    def _(zz):
        finish(zz, TAB, False)

        @pl.loop(0, parts)
        def _(s):
            finish(zz, s, s == 0)


def spread_all(own, own_tab, peers):
    nc, ny = 2, 2
    nz, parts = peers // (nc * ny), 8
    count, width = own.shape[0], own.shape[1]
    return pl.pallas_call(
        functools.partial(spread_kernel, nz, ny, nc, parts),
        out_shape=[
            jax.ShapeDtypeStruct((peers * count, width, width), own.dtype),
            jax.ShapeDtypeStruct((peers,) + own_tab.shape, own_tab.dtype),
        ],
        in_specs=[pl.BlockSpec(memory_space=pl.ANY)] * 2,
        out_specs=[pl.BlockSpec(memory_space=pl.ANY)] * 2,
        scratch_shapes=[
            pltpu.SemaphoreType.DMA((4, nz * ny, parts + 1)),
            pltpu.SemaphoreType.DMA((peers, parts + 1)),
            pltpu.SemaphoreType.DMA((2,)),
        ],
        compiler_params=pltpu.CompilerParams(collective_id=0, has_side_effects=True),
    )(own, own_tab)


def rebuild_kernel(terms, scale, row, tl, tf, rix, tabs, blk, whole, cot, fresh, square, right0, right1, square2, sqcot, sendback, acc, cube, both, racc, parts):
    count, requests = fresh.shape[0], right0.shape[0]
    me = row[0]

    def term_ids(b):
        group, at = b // count, (b % count) * 2 * terms
        lefts = [group * count + tabs[group, 0, at + t] for t in range(terms)]
        rights = [blk[group * requests + tabs[group, 0, at + terms + t]] for t in range(terms)]
        return lefts, rights

    def product(left, lefts, rights):
        lhs = jnp.concatenate([left[i] for i in lefts], axis=1)
        rhs = jnp.concatenate([whole[i] for i in rights], axis=0)
        return scale * dot(lhs, rhs)

    @pl.loop(0, requests, unroll=2)
    def _(q):
        b = blk[me * requests + q]
        right0[q] = whole[b]
        lefts, _ = term_ids(b)
        for t, i in enumerate(lefts + [b]):
            parts[q * (terms + 1) + t] = product(whole, *term_ids(i)).astype(BF16)

    @pl.loop(0, requests, unroll=8)
    def _(q):
        _, rights = term_ids(blk[me * requests + q])
        at = q * (terms + 1)
        cubed = product(parts, [at + t for t in range(terms)], rights)
        right1[q] = (3.0 * parts[at + terms].astype(F32) - 2.0 * cubed).astype(BF16)

    square_phase(terms, scale, tl, tf, whole.at[pl.ds(me * count, count)], right0, square)
    fresh_phase(terms, scale, tl, tf, square, right0, fresh)
    reverse_kernel(terms, scale, tl, tf, tf, rix, fresh, right1, cot, square2, sqcot, sendback, acc, cube, both, racc)


def call(kernel, prefetch, arrays, outs, scratch=(), flops=0):
    whole = pl.BlockSpec(memory_space=pltpu.VMEM)
    smem = pl.BlockSpec(memory_space=pltpu.SMEM)
    moved = sum(a.size * a.dtype.itemsize for a in arrays)
    return pl.pallas_call(
        kernel,
        out_shape=outs,
        in_specs=[smem] * len(prefetch) + [whole] * len(arrays),
        out_specs=[whole] * len(outs),
        scratch_shapes=list(scratch),
        cost_estimate=pl.CostEstimate(flops=flops, bytes_accessed=moved, transcendentals=0),
        compiler_params=pltpu.CompilerParams(vmem_limit_bytes=VMEM_LIMIT),
    )(*prefetch, *arrays)


def body(density_guess, cotangent, term_left, term_fetch, req_owner, req_slot):
    peer_count = lax.axis_size("row")
    own_index = lax.axis_index("row")
    request_count = req_owner.shape[0] // peer_count
    slot_count = max(2, 2 * request_count // peer_count)
    blocks, width = density_guess.shape[0], density_guess.shape[1]
    terms = term_left.shape[1]
    scale = float(width * terms) ** (-0.5)
    send_index, receive_index = owner_tables(
        req_owner, req_slot, own_index, peer_count, slot_count, request_count
    )
    slots = peer_count * slot_count
    tl, tf = term_left, term_fetch

    def shape(n, dtype):
        return jax.ShapeDtypeStruct((n, width, width), dtype)

    def exchange(x):
        return lax.all_to_all(x, "row", split_axis=0, concat_axis=0, tiled=True)

    work = 2 * blocks * terms * width ** 3
    common = [
        pltpu.VMEM((blocks, width, width), F32),
        pltpu.VMEM((blocks, width, width), BF16),
        pltpu.VMEM((blocks, width, 2 * width), BF16),
        pltpu.VMEM((request_count, width, width), F32),
    ]
    if peer_count * blocks * width * width * 2 <= GATHER_BYTES and peer_count % 4 == 0:
        tr = tf
        own_tab = jnp.concatenate([term_left, term_fetch], axis=1).reshape(1, -1)
        own_tab = jnp.broadcast_to(own_tab, (8, own_tab.shape[1]))
        named = req_owner[:, 0] * blocks + req_slot
        whole, tabs = spread_all(density_guess, own_tab, peer_count)
        first, square1, right0, right1, square2, sqcot2, back2 = call(
            functools.partial(rebuild_kernel, terms, scale),
            [own_index.reshape(1), tl, tf, receive_index, tabs, named], [whole, cotangent],
            [shape(blocks, BF16), shape(blocks, BF16), shape(request_count, BF16), shape(request_count, BF16),
             shape(blocks, BF16), shape(blocks, BF16), shape(slots, BF16)],
            common + [pltpu.VMEM((request_count * (terms + 1), width, width), BF16)], flops=(peer_count + 6) * work)
    else:
        tr = receive_index[tf]
        (out0,) = call(gather_kernel, [send_index], [density_guess], [shape(slots, BF16)])
        right0 = exchange(out0)
        first, square1, out1 = call(
            functools.partial(forward_kernel, terms, scale), [tl, tr, send_index], [density_guess, right0],
            [shape(blocks, BF16), shape(blocks, BF16), shape(slots, BF16)], flops=2 * work)
        right1 = exchange(out1)
        square2, sqcot2, back2 = call(
            functools.partial(reverse_kernel, terms, scale), [tl, tr, tf, receive_index],
            [first, right1, cotangent],
            [shape(blocks, BF16), shape(blocks, BF16), shape(slots, BF16)], common, flops=4 * work)
    returned2 = exchange(back2)
    (second,) = call(
        functools.partial(fresh_phase, terms, scale), [tl, tr], [square2, right1], [shape(blocks, BF16)], flops=work)
    local = functools.partial(local_kernel, terms, scale)
    (local2,) = call(local, [tl, tr], [sqcot2, right1], [shape(blocks, F32)], flops=work)
    sqcot1, back1 = call(
        functools.partial(chained_kernel, terms, scale),
        [tl, tr, tf, receive_index, send_index],
        [density_guess, square1, right0, local2, returned2],
        [shape(blocks, BF16), shape(slots, BF16)],
        common + [pltpu.VMEM((blocks, width, width), BF16)], flops=3 * work)
    returned1 = exchange(back1)
    (local1,) = call(local, [tl, tr], [sqcot1, right0], [shape(blocks, F32)], flops=work)
    (grad,) = call(final_kernel, [send_index], [local1, returned1], [shape(blocks, F32)])
    return (second, grad)


def solution(mesh):
    placed = (
        P(("groups", "row"), None, None),
        P(("groups", "row"), None, None),
        P(("groups", "row"), None),
        P(("groups", "row"), None),
        P("groups", None),
        P("groups"),
    )
    return jax.shard_map(
        body,
        mesh=mesh,
        in_specs=placed,
        out_specs=(P(("groups", "row"), None, None), P(("groups", "row"), None, None)),
        check_vma=False,
    )
```

```python
import functools

import jax
import jax.numpy as jnp
from jax import lax
from jax.experimental import pallas as pl
from jax.experimental.pallas import tpu as pltpu
from jax.sharding import PartitionSpec as P

F32 = jnp.float32
BF16 = jnp.bfloat16
VMEM_LIMIT = 56 * 1024 * 1024
GATHER_BYTES = 16 * 1024 * 1024


def owner_tables(req_owner, req_slot, own_index, peer_count, slot_count, request_count):
    owners_all = req_owner[:, 0].reshape(peer_count, request_count)
    slots_all = req_slot.reshape(peer_count, request_count)
    mine = owners_all == own_index
    ranks = jnp.cumsum(mine.astype(jnp.int32), axis=1) - 1
    slot_ids = jnp.arange(slot_count, dtype=jnp.int32)
    chosen = mine[:, None, :] & (ranks[:, None, :] == slot_ids[None, :, None])
    send_index = jnp.sum(jnp.where(chosen, slots_all[:, None, :], 0), axis=2).reshape(-1)
    own_owners = lax.dynamic_slice_in_dim(req_owner[:, 0], own_index * request_count, request_count)
    request_ids = jnp.arange(request_count, dtype=jnp.int32)
    earlier = (own_owners[:, None] == own_owners[None, :]) & (
        request_ids[None, :] < request_ids[:, None]
    )
    own_rank = jnp.sum(earlier.astype(jnp.int32), axis=1)
    receive_index = own_owners * slot_count + own_rank
    return (send_index, receive_index)


class Rows:
    def __init__(self, tab, stride, first):
        self.tab, self.stride, self.first = tab, stride, first

    def __getitem__(self, at):
        return self.tab[0, at[0] * self.stride + self.first + at[1]]


def with_terms(kernel, terms, groups, scale):
    def run(tab, *rest):
        tl, tf, tr = (Rows(tab, groups * terms, i * terms) for i in (0, 1, groups - 1))
        kernel(terms, scale, tl, tr, tf, *rest)

    return run


def dot(a, b):
    return jnp.dot(a, b, preferred_element_type=F32)


def dot_rt(a, b):
    return lax.dot_general(a, b, (((1,), (1,)), ((), ())), preferred_element_type=F32)


def forward_sums(left, right, tl, tr, b, terms):
    lhs = jnp.concatenate([left[tl[b, t]] for t in range(terms)], axis=1)
    rhs = jnp.concatenate([right[tr[b, t]] for t in range(terms)], axis=0)
    return dot(lhs, rhs)


def left_adjoint(cots, right, tl, tr, acc, terms):
    acc[...] = jnp.zeros_like(acc)

    @pl.loop(0, cots.shape[0], unroll=8)
    def _(b):
        rhs = jnp.concatenate([right[tr[b, t]] for t in range(terms)], axis=0)
        piece = dot_rt(cots[b], rhs)
        width = cots.shape[2]
        for t in range(terms):
            acc[tl[b, t]] += piece[:, t * width:(t + 1) * width]


def gather_kernel(index, blocks, out):
    @pl.loop(0, out.shape[0], unroll=4)
    def _(s):
        out[s] = blocks[index[s]]


def square_phase(terms, scale, tl, tr, tf, dens, right, square):
    @pl.loop(0, dens.shape[0], unroll=16)
    def _(b):
        square[b] = (scale * forward_sums(dens, right, tl, tr, b, terms)).astype(BF16)


def fresh_phase(terms, scale, tl, tr, tf, square, right, fresh):
    @pl.loop(0, square.shape[0], unroll=16)
    def _(b):
        cube = scale * forward_sums(square, right, tl, tr, b, terms)
        fresh[b] = (3.0 * square[b].astype(F32) - 2.0 * cube).astype(BF16)


def forward_kernel(terms, scale, tl, tr, tf, index, dens, right, fresh, square, out):
    square_phase(terms, scale, tl, tr, tf, dens, right, square)
    fresh_phase(terms, scale, tl, tr, tf, square, right, fresh)
    gather_kernel(index, fresh, out)


def cot_phase(terms, scale, tl, tr, tf, row, blk, dens, square, right, cot, sqcot, sendback, acc, cube, both, racc, counts):
    blocks, width = dens.shape[0], dens.shape[2]

    @pl.loop(0, blocks, unroll=4)
    def _(b):
        cube[b] = (-2.0 * cot[b].astype(F32)).astype(BF16)
        both[b] = jnp.concatenate([square[b].T, dens[b].T], axis=1)

    left_adjoint(cube, right, tl, tr, acc, terms)

    @pl.loop(0, blocks, unroll=4)
    def _(b):
        sqcot[b] = (3.0 * cot[b].astype(F32) + scale * acc[b]).astype(BF16)

    racc[...] = jnp.zeros_like(racc)

    @pl.loop(0, blocks, unroll=8)
    def _(b):
        lhs = jnp.concatenate([both[tl[b, t]] for t in range(terms)], axis=0)
        rhs = jnp.concatenate([cube[b], sqcot[b]], axis=0)
        piece = dot(lhs, rhs)
        for t in range(terms):
            racc[tf[b, t]] += piece[t * width:(t + 1) * width]

    @pl.loop(0, sendback.shape[0], unroll=4)
    def _(s):
        sendback[s] = jnp.zeros(sendback.shape[1:], BF16)

    peers, requests = counts.shape[0], racc.shape[0]

    @pl.loop(0, peers)
    def _(p):
        counts[p] = 0

    @pl.loop(0, requests, unroll=4)
    def _(q):
        owner = blk[row[0] * requests + q] // blocks
        rank = counts[owner]
        counts[owner] = rank + 1
        slot = owner * (sendback.shape[0] // peers) + rank
        sendback[slot] = (scale * racc[q]).astype(BF16)


def reverse_kernel(terms, scale, tl, tr, tf, row, blk, dens, right, cot, square, sqcot, sendback, acc, cube, both, racc, counts):
    square_phase(terms, scale, tl, tr, tf, dens, right, square)
    cot_phase(terms, scale, tl, tr, tf, row, blk, dens, square, right, cot, sqcot, sendback, acc, cube, both, racc, counts)


def collect(index, returned, grad):
    @pl.loop(0, returned.shape[0], unroll=8)
    def _(s):
        grad[index[s]] += returned[s].astype(F32)


def chained_kernel(terms, scale, tl, tr, tf, row, blk, index, dens, square, right, local, returned, sqcot, sendback, acc, cube, both, racc, counts, cot):
    acc[...] = local[...]
    collect(index, returned, acc)
    cot[...] = acc[...].astype(BF16)
    cot_phase(terms, scale, tl, tr, tf, row, blk, dens, square, right, cot, sqcot, sendback, acc, cube, both, racc, counts)


def local_kernel(terms, scale, tl, tr, tf, sqcot, right, grad):
    left_adjoint(sqcot, right, tl, tr, grad, terms)
    grad[...] = scale * grad[...]


def final_kernel(index, local, returned, grad):
    grad[...] = local[...]
    collect(index, returned, grad)


def spread_kernel(nz, ny, nc, parts, own, own_tab, spread, tabs, send_sem, recv_sem, own_sem):
    me = lax.axis_index("row")
    core, y, z = me % nc, (me // nc) % ny, me // (nc * ny)
    count = own.shape[0]
    size = count // parts
    UP, DOWN, ACROSS, TWIN = 0, 1, 2, 3
    steps = {UP: nc * ny, DOWN: -nc * ny}

    def target(way):
        if way == ACROSS:
            return (z * ny + (ny - 1 - y)) * nc + core
        if way == TWIN:
            return (z * ny + y) * nc + (nc - 1 - core)
        return me + steps[way]

    def exists(way):
        return {UP: z + 1 < nz, DOWN: z > 0}[way]

    barrier = pltpu.get_barrier_semaphore()

    def greet(way):
        pl.semaphore_signal(barrier, inc=1, device_id={"row": target(way)}, device_id_type=pl.DeviceIdType.MESH)

    for way in (UP, DOWN):
        pl.when(exists(way))(functools.partial(greet, way))
    for way in (ACROSS, TWIN):
        greet(way)
    pl.semaphore_wait(barrier, 2 + (z + 1 < nz).astype(jnp.int32) + (z > 0).astype(jnp.int32))

    TAB = parts

    def place_of(origin, s):
        if s is TAB:
            return tabs.at[origin]
        return spread.at[pl.ds(origin * count + s * size, size)]

    def copy(way, zz, yy, s, from_own=False):
        origin = (zz * ny + yy) * nc + core
        place = source = place_of(origin, s)
        if from_own:
            source = own_tab if s is TAB else own.at[pl.ds(s * size, size)]
        return pltpu.make_async_remote_copy(
            src_ref=source, dst_ref=place,
            send_sem=send_sem.at[way, zz * ny + yy, s], recv_sem=recv_sem.at[origin, s],
            device_id={"row": target(way)}, device_id_type=pl.DeviceIdType.MESH)

    def arrived(zz, yy, s, plane):
        origin = (zz * ny + yy) * nc + plane
        place = place_of(origin, s)
        pltpu.make_async_remote_copy(
            src_ref=place, dst_ref=place,
            send_sem=send_sem.at[TWIN, 0, 0], recv_sem=recv_sem.at[origin, s],
            device_id={"row": target(TWIN)}, device_id_type=pl.DeviceIdType.MESH).wait_recv()

    def maybe(way, act):
        pl.when(exists(way))(act)

    kept = pltpu.make_async_copy(own, spread.at[pl.ds(me * count, count)], own_sem.at[0])
    kept.start()
    kept_tab = pltpu.make_async_copy(own_tab, tabs.at[me], own_sem.at[1])
    kept_tab.start()

    def begin(s):
        maybe(UP, lambda: copy(UP, z, y, s, True).start())
        maybe(DOWN, lambda: copy(DOWN, z, y, s, True).start())
        copy(ACROSS, z, y, s, True).start()
        copy(TWIN, z, y, s, True).start()

    begin(TAB)
    pl.loop(0, parts)(begin)

    def along(d, s, yy, cross):
        for way, zz, there in ((UP, z - d, z >= d), (DOWN, z + d, z + d < nz)):
            @pl.when(there)
            def _(way=way, zz=zz):
                arrived(zz, yy, s, core)
                maybe(way, lambda: copy(way, zz, yy, s).start())
                if cross:
                    copy(ACROSS, zz, yy, s).start()
                copy(TWIN, zz, yy, s).start()

    other = ny - 1 - y
    arrived(z, other, 0, core)
    maybe(UP, lambda: copy(UP, z, other, 0).start())
    maybe(DOWN, lambda: copy(DOWN, z, other, 0).start())
    copy(TWIN, z, other, 0).start()

    def crossed(d, s):
        if d == 0:
            arrived(z, other, s, core)
            copy(TWIN, z, other, s).start()
        else:
            for zz, there in ((z - d, z >= d), (z + d, z + d < nz)):
                @pl.when(there)
                def _(zz=zz):
                    arrived(zz, other, s, core)
                    copy(TWIN, zz, other, s).start()

    def drain(d):
        crossed(d, TAB)
        pl.loop(1, parts)(functools.partial(crossed, d))

    for d in range(1, nz):
        along(d, 0, y, False)
        along(d, TAB, y, True)

        @pl.loop(1, parts)
        def _(s):
            along(d, s, y, True)

        along(d, 0, other, False)
        if d == 1:
            drain(0)

    for d in range(1, nz):
        drain(d)

    kept.wait()
    kept_tab.wait()

    @pl.loop(0, nz * ny)
    def _(i):
        arrived(i // ny, i % ny, TAB, nc - 1 - core)

        @pl.loop(0, parts)
        def _(s):
            arrived(i // ny, i % ny, s, nc - 1 - core)

    def sent(way, zz, yy, s):
        copy(way, zz, yy, s).wait_send()

    def finish(zz, s, first):
        for yy in range(ny):
            sent(TWIN, zz, yy, s)

        @pl.when(jnp.logical_or(jnp.logical_not(first), zz == z))
        def _():
            sent(ACROSS, zz, y, s)

        @pl.when((zz <= z) & (z + 1 < nz))
        def _():
            sent(UP, zz, y, s)

        @pl.when((zz >= z) & (z > 0))
        def _():
            sent(DOWN, zz, y, s)

        if s is not TAB:
            @pl.when(first & (zz <= z) & (z + 1 < nz))
            def _():
                sent(UP, zz, other, s)

            @pl.when(first & (zz >= z) & (z > 0))
            def _():
                sent(DOWN, zz, other, s)

    @pl.loop(0, nz)
    def _(zz):
        finish(zz, TAB, False)

        @pl.loop(0, parts)
        def _(s):
            finish(zz, s, s == 0)


def spread_all(own, own_tab, peers):
    nc, ny = 2, 2
    nz, parts = peers // (nc * ny), 8
    count, width = own.shape[0], own.shape[1]
    return pl.pallas_call(
        functools.partial(spread_kernel, nz, ny, nc, parts),
        out_shape=[
            jax.ShapeDtypeStruct((peers * count, width, width), own.dtype),
            jax.ShapeDtypeStruct((peers,) + own_tab.shape, own_tab.dtype),
        ],
        in_specs=[pl.BlockSpec(memory_space=pl.ANY)] * 2,
        out_specs=[pl.BlockSpec(memory_space=pl.ANY)] * 2,
        scratch_shapes=[
            pltpu.SemaphoreType.DMA((4, nz * ny, parts + 1)),
            pltpu.SemaphoreType.DMA((peers, parts + 1)),
            pltpu.SemaphoreType.DMA((2,)),
        ],
        compiler_params=pltpu.CompilerParams(collective_id=0, has_side_effects=True),
    )(own, own_tab)


def rebuild_kernel(terms, scale, tl, tr, tf, row, blk, tabs, whole, cot, fresh, square, right0, right1, square2, sqcot, sendback, acc, cube, both, racc, counts, parts):
    count, requests = fresh.shape[0], right0.shape[0]
    me = row[0]

    def term_ids(b):
        group, at = b // count, (b % count) * 2 * terms
        lefts = [group * count + tabs[group, 0, at + t] for t in range(terms)]
        rights = [blk[group * requests + tabs[group, 0, at + terms + t]] for t in range(terms)]
        return lefts, rights

    def product(left, lefts, rights):
        lhs = jnp.concatenate([left[i] for i in lefts], axis=1)
        rhs = jnp.concatenate([whole[i] for i in rights], axis=0)
        return scale * dot(lhs, rhs)

    @pl.loop(0, requests, unroll=2)
    def _(q):
        b = blk[me * requests + q]
        right0[q] = whole[b]
        lefts, _ = term_ids(b)
        for t, i in enumerate(lefts + [b]):
            parts[q * (terms + 1) + t] = product(whole, *term_ids(i)).astype(BF16)

    @pl.loop(0, requests, unroll=8)
    def _(q):
        _, rights = term_ids(blk[me * requests + q])
        at = q * (terms + 1)
        cubed = product(parts, [at + t for t in range(terms)], rights)
        right1[q] = (3.0 * parts[at + terms].astype(F32) - 2.0 * cubed).astype(BF16)

    square_phase(terms, scale, tl, tr, tf, whole.at[pl.ds(me * count, count)], right0, square)
    fresh_phase(terms, scale, tl, tr, tf, square, right0, fresh)
    reverse_kernel(terms, scale, tl, tr, tf, row, blk, fresh, right1, cot, square2, sqcot, sendback, acc, cube, both, racc, counts)


def call(kernel, prefetch, arrays, outs, scratch=(), flops=0):
    whole = pl.BlockSpec(memory_space=pltpu.VMEM)
    smem = pl.BlockSpec(memory_space=pltpu.SMEM)
    moved = sum(a.size * a.dtype.itemsize for a in arrays)
    return pl.pallas_call(
        kernel,
        out_shape=outs,
        in_specs=[smem] * len(prefetch) + [whole] * len(arrays),
        out_specs=[whole] * len(outs),
        scratch_shapes=list(scratch),
        cost_estimate=pl.CostEstimate(flops=flops, bytes_accessed=moved, transcendentals=0),
        compiler_params=pltpu.CompilerParams(vmem_limit_bytes=VMEM_LIMIT),
    )(*prefetch, *arrays)


def body(density_guess, cotangent, term_left, term_fetch, req_owner, req_slot):
    peer_count = lax.axis_size("row")
    own_index = lax.axis_index("row")
    request_count = req_owner.shape[0] // peer_count
    slot_count = max(2, 2 * request_count // peer_count)
    blocks, width = density_guess.shape[0], density_guess.shape[1]
    terms = term_left.shape[1]
    scale = float(width * terms) ** (-0.5)
    slots = peer_count * slot_count
    row = own_index.reshape(1)
    named = req_owner[:, 0] * blocks + req_slot

    def shape(n, dtype):
        return jax.ShapeDtypeStruct((n, width, width), dtype)

    def exchange(x):
        return lax.all_to_all(x, "row", split_axis=0, concat_axis=0, tiled=True)

    work = 2 * blocks * terms * width ** 3
    common = [
        pltpu.VMEM((blocks, width, width), F32),
        pltpu.VMEM((blocks, width, width), BF16),
        pltpu.VMEM((blocks, width, 2 * width), BF16),
        pltpu.VMEM((request_count, width, width), F32),
        pltpu.SMEM((peer_count,), jnp.int32),
    ]

    def packed(*columns):
        tab = jnp.concatenate(columns, axis=1).reshape(1, -1)
        return jnp.broadcast_to(tab, (8, tab.shape[1]))

    def routes(owner, slot):
        return owner_tables(owner, slot, own_index, peer_count, slot_count, request_count)

    if peer_count * blocks * width * width * 2 <= GATHER_BYTES and peer_count % 4 == 0:
        tab, groups = packed(term_left, term_fetch), 2
        whole, tabs = spread_all(density_guess, tab, peer_count)
        first, square1, right0, right1, square2, sqcot2, back2 = call(
            with_terms(rebuild_kernel, terms, groups, scale),
            [tab, row, named, tabs], [whole, cotangent],
            [shape(blocks, BF16), shape(blocks, BF16), shape(request_count, BF16), shape(request_count, BF16),
             shape(blocks, BF16), shape(blocks, BF16), shape(slots, BF16)],
            common + [pltpu.VMEM((request_count * (terms + 1), width, width), BF16)], flops=(peer_count + 6) * work)
        owner, slot, back2 = lax.optimization_barrier((req_owner, req_slot, back2))
        send_index, _ = routes(owner, slot)
    else:
        send_index, receive_index = routes(req_owner, req_slot)
        tab, groups = packed(term_left, term_fetch, receive_index[term_fetch]), 3
        (out0,) = call(gather_kernel, [send_index], [density_guess], [shape(slots, BF16)])
        right0 = exchange(out0)
        first, square1, out1 = call(
            with_terms(forward_kernel, terms, groups, scale), [tab, send_index], [density_guess, right0],
            [shape(blocks, BF16), shape(blocks, BF16), shape(slots, BF16)], flops=2 * work)
        right1 = exchange(out1)
        square2, sqcot2, back2 = call(
            with_terms(reverse_kernel, terms, groups, scale), [tab, row, named],
            [first, right1, cotangent],
            [shape(blocks, BF16), shape(blocks, BF16), shape(slots, BF16)], common, flops=4 * work)
    returned2 = exchange(back2)
    (second,) = call(
        with_terms(fresh_phase, terms, groups, scale), [tab], [square2, right1], [shape(blocks, BF16)], flops=work)
    local = with_terms(local_kernel, terms, groups, scale)
    (local2,) = call(local, [tab], [sqcot2, right1], [shape(blocks, F32)], flops=work)
    sqcot1, back1 = call(
        with_terms(chained_kernel, terms, groups, scale), [tab, row, named, send_index],
        [density_guess, square1, right0, local2, returned2],
        [shape(blocks, BF16), shape(slots, BF16)],
        common + [pltpu.VMEM((blocks, width, width), BF16)], flops=3 * work)
    returned1 = exchange(back1)
    (local1,) = call(local, [tab], [sqcot1, right0], [shape(blocks, F32)], flops=work)
    (grad,) = call(final_kernel, [send_index], [local1, returned1], [shape(blocks, F32)])
    return (second, grad)


def solution(mesh):
    placed = (
        P(("groups", "row"), None, None),
        P(("groups", "row"), None, None),
        P(("groups", "row"), None),
        P(("groups", "row"), None),
        P("groups", None),
        P("groups"),
    )
    return jax.shard_map(
        body,
        mesh=mesh,
        in_specs=placed,
        out_specs=(P(("groups", "row"), None, None), P(("groups", "row"), None, None)),
        check_vma=False,
    )
```

```python
import functools

import jax
import jax.numpy as jnp
from jax import lax
from jax.experimental import pallas as pl
from jax.experimental.pallas import tpu as pltpu
from jax.sharding import PartitionSpec as P

F32 = jnp.float32
BF16 = jnp.bfloat16
VMEM_LIMIT = 56 * 1024 * 1024
LANDINGS = 4
GATHER_BYTES = 16 * 1024 * 1024


def owner_tables(req_owner, req_slot, own_index, peer_count, slot_count, request_count):
    owners_all = req_owner[:, 0].reshape(peer_count, request_count)
    slots_all = req_slot.reshape(peer_count, request_count)
    mine = owners_all == own_index
    ranks = jnp.cumsum(mine.astype(jnp.int32), axis=1) - 1
    slot_ids = jnp.arange(slot_count, dtype=jnp.int32)
    chosen = mine[:, None, :] & (ranks[:, None, :] == slot_ids[None, :, None])
    send_index = jnp.sum(jnp.where(chosen, slots_all[:, None, :], 0), axis=2).reshape(-1)
    own_owners = lax.dynamic_slice_in_dim(req_owner[:, 0], own_index * request_count, request_count)
    request_ids = jnp.arange(request_count, dtype=jnp.int32)
    earlier = (own_owners[:, None] == own_owners[None, :]) & (
        request_ids[None, :] < request_ids[:, None]
    )
    own_rank = jnp.sum(earlier.astype(jnp.int32), axis=1)
    receive_index = own_owners * slot_count + own_rank
    return (send_index, receive_index)


class Rows:
    def __init__(self, tab, stride, first):
        self.tab, self.stride, self.first = tab, stride, first

    def __getitem__(self, at):
        return self.tab[0, at[0] * self.stride + self.first + at[1]]


def with_terms(kernel, terms, groups, scale):
    def run(tab, *rest):
        tl, tf, tr = (Rows(tab, groups * terms, i * terms) for i in (0, 1, groups - 1))
        kernel(terms, scale, tl, tr, tf, *rest)

    return run


def dot(a, b):
    return jnp.dot(a, b, preferred_element_type=F32)


def dot_rt(a, b):
    return lax.dot_general(a, b, (((1,), (1,)), ((), ())), preferred_element_type=F32)


def forward_sums(left, right, tl, tr, b, terms):
    lhs = jnp.concatenate([left[tl[b, t]] for t in range(terms)], axis=1)
    rhs = jnp.concatenate([right[tr[b, t]] for t in range(terms)], axis=0)
    return dot(lhs, rhs)


def left_adjoint(cots, right, tl, tr, acc, terms):
    acc[...] = jnp.zeros_like(acc)

    @pl.loop(0, cots.shape[0], unroll=8)
    def _(b):
        rhs = jnp.concatenate([right[tr[b, t]] for t in range(terms)], axis=0)
        piece = dot_rt(cots[b], rhs)
        width = cots.shape[2]
        for t in range(terms):
            acc[tl[b, t]] += piece[:, t * width:(t + 1) * width]


def gather_kernel(index, blocks, out):
    @pl.loop(0, out.shape[0], unroll=4)
    def _(s):
        out[s] = blocks[index[s]]


def square_phase(terms, scale, tl, tr, tf, dens, right, square):
    @pl.loop(0, dens.shape[0], unroll=16)
    def _(b):
        square[b] = (scale * forward_sums(dens, right, tl, tr, b, terms)).astype(BF16)


def fresh_phase(terms, scale, tl, tr, tf, square, right, fresh):
    @pl.loop(0, square.shape[0], unroll=16)
    def _(b):
        cube = scale * forward_sums(square, right, tl, tr, b, terms)
        fresh[b] = (3.0 * square[b].astype(F32) - 2.0 * cube).astype(BF16)


def forward_kernel(terms, scale, tl, tr, tf, index, dens, right, fresh, square, out):
    square_phase(terms, scale, tl, tr, tf, dens, right, square)
    fresh_phase(terms, scale, tl, tr, tf, square, right, fresh)
    gather_kernel(index, fresh, out)


def turn(dens, square, both):
    @pl.loop(0, dens.shape[0], unroll=8)
    def _(b):
        both[b] = jnp.concatenate([square[b].T, dens[b].T], axis=1)


def cot_phase(terms, scale, tl, tr, tf, row, blk, dens, right, cot, sqcot, sendback, acc, cube, both, racc, counts):
    blocks, width = dens.shape[0], dens.shape[2]

    @pl.loop(0, blocks, unroll=4)
    def _(b):
        cube[b] = (-2.0 * cot[b].astype(F32)).astype(BF16)

    left_adjoint(cube, right, tl, tr, acc, terms)

    @pl.loop(0, blocks, unroll=4)
    def _(b):
        sqcot[b] = (3.0 * cot[b].astype(F32) + scale * acc[b]).astype(BF16)

    racc[...] = jnp.zeros_like(racc)

    @pl.loop(0, blocks, unroll=8)
    def _(b):
        lhs = jnp.concatenate([both[tl[b, t]] for t in range(terms)], axis=0)
        rhs = jnp.concatenate([cube[b], sqcot[b]], axis=0)
        piece = dot(lhs, rhs)
        for t in range(terms):
            racc[tf[b, t]] += piece[t * width:(t + 1) * width]

    @pl.loop(0, sendback.shape[0], unroll=4)
    def _(s):
        sendback[s] = jnp.zeros(sendback.shape[1:], BF16)

    peers, requests = counts.shape[0], racc.shape[0]

    @pl.loop(0, peers)
    def _(p):
        counts[p] = 0

    @pl.loop(0, requests, unroll=4)
    def _(q):
        owner = blk[row[0] * requests + q] // blocks
        rank = counts[owner]
        counts[owner] = rank + 1
        slot = owner * (sendback.shape[0] // peers) + rank
        sendback[slot] = (scale * racc[q]).astype(BF16)


def reverse_kernel(terms, scale, tl, tr, tf, row, blk, dens, right, cot, square, sqcot, sendback, acc, cube, both, racc, counts):
    square_phase(terms, scale, tl, tr, tf, dens, right, square)
    turn(dens, square, both)
    cot_phase(terms, scale, tl, tr, tf, row, blk, dens, right, cot, sqcot, sendback, acc, cube, both, racc, counts)


def collect(index, returned, landing, sems, grad, before):
    size = returned.shape[0] // LANDINGS

    def fetch(i):
        span = pl.ds(i * size, size)
        return pltpu.make_async_copy(returned.at[span], landing.at[span], sems.at[i])

    for i in range(LANDINGS):
        fetch(i).start()
    before()
    for i in range(LANDINGS):
        fetch(i).wait()

        @pl.loop(0, size, unroll=8)
        def _(s):
            grad[index[i * size + s]] += landing[i * size + s].astype(F32)


def chained_kernel(terms, scale, tl, tr, tf, row, blk, index, dens, square, right, local, returned, sqcot, sendback, acc, cube, both, racc, counts, cot, landing, sems):
    def before():
        acc[...] = local[...]
        turn(dens, square, both)

    collect(index, returned, landing, sems, acc, before)
    cot[...] = acc[...].astype(BF16)
    cot_phase(terms, scale, tl, tr, tf, row, blk, dens, right, cot, sqcot, sendback, acc, cube, both, racc, counts)


def local_kernel(terms, scale, tl, tr, tf, sqcot, right, grad):
    left_adjoint(sqcot, right, tl, tr, grad, terms)
    grad[...] = scale * grad[...]


def final_kernel(index, local, returned, grad, landing, sems):
    def before():
        grad[...] = local[...]

    collect(index, returned, landing, sems, grad, before)


def spread_kernel(nz, ny, nc, parts, own, own_tab, spread, tabs, send_sem, recv_sem, own_sem):
    me = lax.axis_index("row")
    core, y, z = me % nc, (me // nc) % ny, me // (nc * ny)
    count = own.shape[0]
    size = count // parts
    UP, DOWN, ACROSS, TWIN = 0, 1, 2, 3
    steps = {UP: nc * ny, DOWN: -nc * ny}

    def target(way):
        if way == ACROSS:
            return (z * ny + (ny - 1 - y)) * nc + core
        if way == TWIN:
            return (z * ny + y) * nc + (nc - 1 - core)
        return me + steps[way]

    def exists(way):
        return {UP: z + 1 < nz, DOWN: z > 0}[way]

    barrier = pltpu.get_barrier_semaphore()

    def greet(way):
        pl.semaphore_signal(barrier, inc=1, device_id={"row": target(way)}, device_id_type=pl.DeviceIdType.MESH)

    for way in (UP, DOWN):
        pl.when(exists(way))(functools.partial(greet, way))
    for way in (ACROSS, TWIN):
        greet(way)
    pl.semaphore_wait(barrier, 2 + (z + 1 < nz).astype(jnp.int32) + (z > 0).astype(jnp.int32))

    TAB = parts

    def place_of(origin, s):
        if s is TAB:
            return tabs.at[origin]
        return spread.at[pl.ds(origin * count + s * size, size)]

    def copy(way, zz, yy, s, from_own=False):
        origin = (zz * ny + yy) * nc + core
        place = source = place_of(origin, s)
        if from_own:
            source = own_tab if s is TAB else own.at[pl.ds(s * size, size)]
        return pltpu.make_async_remote_copy(
            src_ref=source, dst_ref=place,
            send_sem=send_sem.at[way, zz * ny + yy, s], recv_sem=recv_sem.at[origin, s],
            device_id={"row": target(way)}, device_id_type=pl.DeviceIdType.MESH)

    def arrived(zz, yy, s, plane):
        origin = (zz * ny + yy) * nc + plane
        place = place_of(origin, s)
        pltpu.make_async_remote_copy(
            src_ref=place, dst_ref=place,
            send_sem=send_sem.at[TWIN, 0, 0], recv_sem=recv_sem.at[origin, s],
            device_id={"row": target(TWIN)}, device_id_type=pl.DeviceIdType.MESH).wait_recv()

    def maybe(way, act):
        pl.when(exists(way))(act)

    kept = pltpu.make_async_copy(own, spread.at[pl.ds(me * count, count)], own_sem.at[0])
    kept.start()
    kept_tab = pltpu.make_async_copy(own_tab, tabs.at[me], own_sem.at[1])
    kept_tab.start()

    def begin(s):
        maybe(UP, lambda: copy(UP, z, y, s, True).start())
        maybe(DOWN, lambda: copy(DOWN, z, y, s, True).start())
        copy(ACROSS, z, y, s, True).start()
        copy(TWIN, z, y, s, True).start()

    begin(TAB)
    pl.loop(0, parts)(begin)

    def along(d, s, yy, cross):
        for way, zz, there in ((UP, z - d, z >= d), (DOWN, z + d, z + d < nz)):
            @pl.when(there)
            def _(way=way, zz=zz):
                arrived(zz, yy, s, core)
                maybe(way, lambda: copy(way, zz, yy, s).start())
                if cross:
                    copy(ACROSS, zz, yy, s).start()
                copy(TWIN, zz, yy, s).start()

    other = ny - 1 - y
    arrived(z, other, 0, core)
    maybe(UP, lambda: copy(UP, z, other, 0).start())
    maybe(DOWN, lambda: copy(DOWN, z, other, 0).start())
    copy(TWIN, z, other, 0).start()

    def crossed(d, s):
        if d == 0:
            arrived(z, other, s, core)
            copy(TWIN, z, other, s).start()
        else:
            for zz, there in ((z - d, z >= d), (z + d, z + d < nz)):
                @pl.when(there)
                def _(zz=zz):
                    arrived(zz, other, s, core)
                    copy(TWIN, zz, other, s).start()

    def drain(d):
        crossed(d, TAB)
        pl.loop(1, parts)(functools.partial(crossed, d))

    for d in range(1, nz):
        along(d, 0, y, False)
        along(d, TAB, y, True)

        @pl.loop(1, parts)
        def _(s):
            along(d, s, y, True)

        along(d, 0, other, False)
        if d == 1:
            drain(0)

    for d in range(1, nz):
        drain(d)

    kept.wait()
    kept_tab.wait()

    @pl.loop(0, nz * ny)
    def _(i):
        arrived(i // ny, i % ny, TAB, nc - 1 - core)

        @pl.loop(0, parts)
        def _(s):
            arrived(i // ny, i % ny, s, nc - 1 - core)

    def sent(way, zz, yy, s):
        copy(way, zz, yy, s).wait_send()

    def finish(zz, s, first):
        for yy in range(ny):
            sent(TWIN, zz, yy, s)

        @pl.when(jnp.logical_or(jnp.logical_not(first), zz == z))
        def _():
            sent(ACROSS, zz, y, s)

        @pl.when((zz <= z) & (z + 1 < nz))
        def _():
            sent(UP, zz, y, s)

        @pl.when((zz >= z) & (z > 0))
        def _():
            sent(DOWN, zz, y, s)

        if s is not TAB:
            @pl.when(first & (zz <= z) & (z + 1 < nz))
            def _():
                sent(UP, zz, other, s)

            @pl.when(first & (zz >= z) & (z > 0))
            def _():
                sent(DOWN, zz, other, s)

    @pl.loop(0, nz)
    def _(zz):
        finish(zz, TAB, False)

        @pl.loop(0, parts)
        def _(s):
            finish(zz, s, s == 0)


def spread_all(own, own_tab, peers):
    nc, ny = 2, 2
    nz, parts = peers // (nc * ny), 8
    count, width = own.shape[0], own.shape[1]
    return pl.pallas_call(
        functools.partial(spread_kernel, nz, ny, nc, parts),
        out_shape=[
            jax.ShapeDtypeStruct((peers * count, width, width), own.dtype),
            jax.ShapeDtypeStruct((peers,) + own_tab.shape, own_tab.dtype),
        ],
        in_specs=[pl.BlockSpec(memory_space=pl.ANY)] * 2,
        out_specs=[pl.BlockSpec(memory_space=pl.ANY)] * 2,
        scratch_shapes=[
            pltpu.SemaphoreType.DMA((4, nz * ny, parts + 1)),
            pltpu.SemaphoreType.DMA((peers, parts + 1)),
            pltpu.SemaphoreType.DMA((2,)),
        ],
        compiler_params=pltpu.CompilerParams(collective_id=0, has_side_effects=True),
    )(own, own_tab)


def rebuild_kernel(terms, scale, tl, tr, tf, row, blk, tabs, whole, cot, fresh, square, right0, right1, square2, sqcot, sendback, acc, cube, both, racc, counts, parts):
    count, requests = fresh.shape[0], right0.shape[0]
    me = row[0]

    def term_ids(b):
        group, at = b // count, (b % count) * 2 * terms
        lefts = [group * count + tabs[group, 0, at + t] for t in range(terms)]
        rights = [blk[group * requests + tabs[group, 0, at + terms + t]] for t in range(terms)]
        return lefts, rights

    def product(left, lefts, rights):
        lhs = jnp.concatenate([left[i] for i in lefts], axis=1)
        rhs = jnp.concatenate([whole[i] for i in rights], axis=0)
        return scale * dot(lhs, rhs)

    @pl.loop(0, requests, unroll=4)
    def _(q):
        b = blk[me * requests + q]
        right0[q] = whole[b]
        lefts, _ = term_ids(b)
        for t, i in enumerate(lefts + [b]):
            parts[q * (terms + 1) + t] = product(whole, *term_ids(i)).astype(BF16)

    @pl.loop(0, requests, unroll=8)
    def _(q):
        _, rights = term_ids(blk[me * requests + q])
        at = q * (terms + 1)
        cubed = product(parts, [at + t for t in range(terms)], rights)
        right1[q] = (3.0 * parts[at + terms].astype(F32) - 2.0 * cubed).astype(BF16)

    square_phase(terms, scale, tl, tr, tf, whole.at[pl.ds(me * count, count)], right0, square)
    fresh_phase(terms, scale, tl, tr, tf, square, right0, fresh)
    reverse_kernel(terms, scale, tl, tr, tf, row, blk, fresh, right1, cot, square2, sqcot, sendback, acc, cube, both, racc, counts)


def call(kernel, prefetch, arrays, outs, scratch=(), flops=0, left_out=0):
    whole = pl.BlockSpec(memory_space=pltpu.VMEM)
    smem = pl.BlockSpec(memory_space=pltpu.SMEM)
    moved = sum(a.size * a.dtype.itemsize for a in arrays)
    return pl.pallas_call(
        kernel,
        out_shape=outs,
        in_specs=[smem] * len(prefetch) + [whole] * (len(arrays) - left_out) + [pl.BlockSpec(memory_space=pltpu.HBM)] * left_out,
        out_specs=[whole] * len(outs),
        scratch_shapes=list(scratch),
        cost_estimate=pl.CostEstimate(flops=flops, bytes_accessed=moved, transcendentals=0),
        compiler_params=pltpu.CompilerParams(vmem_limit_bytes=VMEM_LIMIT),
    )(*prefetch, *arrays)


def body(density_guess, cotangent, term_left, term_fetch, req_owner, req_slot):
    peer_count = lax.axis_size("row")
    own_index = lax.axis_index("row")
    request_count = req_owner.shape[0] // peer_count
    slot_count = max(2, 2 * request_count // peer_count)
    blocks, width = density_guess.shape[0], density_guess.shape[1]
    terms = term_left.shape[1]
    scale = float(width * terms) ** (-0.5)
    slots = peer_count * slot_count
    row = own_index.reshape(1)
    named = req_owner[:, 0] * blocks + req_slot

    def shape(n, dtype):
        return jax.ShapeDtypeStruct((n, width, width), dtype)

    def exchange(x):
        return lax.all_to_all(x, "row", split_axis=0, concat_axis=0, tiled=True)

    work = 2 * blocks * terms * width ** 3
    common = [
        pltpu.VMEM((blocks, width, width), F32),
        pltpu.VMEM((blocks, width, width), BF16),
        pltpu.VMEM((blocks, width, 2 * width), BF16),
        pltpu.VMEM((request_count, width, width), F32),
        pltpu.SMEM((peer_count,), jnp.int32),
    ]

    landing = [pltpu.VMEM((slots, width, width), BF16), pltpu.SemaphoreType.DMA((LANDINGS,))]

    def packed(*columns):
        tab = jnp.concatenate(columns, axis=1).reshape(1, -1)
        return jnp.broadcast_to(tab, (8, tab.shape[1]))

    def routes(owner, slot):
        return owner_tables(owner, slot, own_index, peer_count, slot_count, request_count)

    if peer_count * blocks * width * width * 2 <= GATHER_BYTES and peer_count % 4 == 0:
        tab, groups = packed(term_left, term_fetch), 2
        whole, tabs = spread_all(density_guess, tab, peer_count)
        first, square1, right0, right1, square2, sqcot2, back2 = call(
            with_terms(rebuild_kernel, terms, groups, scale),
            [tab, row, named, tabs], [whole, cotangent],
            [shape(blocks, BF16), shape(blocks, BF16), shape(request_count, BF16), shape(request_count, BF16),
             shape(blocks, BF16), shape(blocks, BF16), shape(slots, BF16)],
            common + [pltpu.VMEM((request_count * (terms + 1), width, width), BF16)], flops=(peer_count + 6) * work)
        owner, slot, back2 = lax.optimization_barrier((req_owner, req_slot, back2))
        send_index, _ = routes(owner, slot)
    else:
        send_index, receive_index = routes(req_owner, req_slot)
        tab, groups = packed(term_left, term_fetch, receive_index[term_fetch]), 3
        (out0,) = call(gather_kernel, [send_index], [density_guess], [shape(slots, BF16)])
        right0 = exchange(out0)
        first, square1, out1 = call(
            with_terms(forward_kernel, terms, groups, scale), [tab, send_index], [density_guess, right0],
            [shape(blocks, BF16), shape(blocks, BF16), shape(slots, BF16)], flops=2 * work)
        right1 = exchange(out1)
        square2, sqcot2, back2 = call(
            with_terms(reverse_kernel, terms, groups, scale), [tab, row, named],
            [first, right1, cotangent],
            [shape(blocks, BF16), shape(blocks, BF16), shape(slots, BF16)], common, flops=4 * work)
    returned2 = exchange(back2)
    (second,) = call(
        with_terms(fresh_phase, terms, groups, scale), [tab], [square2, right1], [shape(blocks, BF16)], flops=work)
    local = with_terms(local_kernel, terms, groups, scale)
    (local2,) = call(local, [tab], [sqcot2, right1], [shape(blocks, F32)], flops=work)
    sqcot1, back1 = call(
        with_terms(chained_kernel, terms, groups, scale), [tab, row, named, send_index],
        [density_guess, square1, right0, local2, returned2],
        [shape(blocks, BF16), shape(slots, BF16)],
        common + [pltpu.VMEM((blocks, width, width), BF16)] + landing, flops=3 * work, left_out=1)
    returned1 = exchange(back1)
    (local1,) = call(local, [tab], [sqcot1, right0], [shape(blocks, F32)], flops=work)
    (grad,) = call(final_kernel, [send_index], [local1, returned1], [shape(blocks, F32)], landing, left_out=1)
    return (second, grad)


def solution(mesh):
    placed = (
        P(("groups", "row"), None, None),
        P(("groups", "row"), None, None),
        P(("groups", "row"), None),
        P(("groups", "row"), None),
        P("groups", None),
        P("groups"),
    )
    return jax.shard_map(
        body,
        mesh=mesh,
        in_specs=placed,
        out_specs=(P(("groups", "row"), None, None), P(("groups", "row"), None, None)),
        check_vma=False,
    )
```

```python
import functools
import math

import jax
import jax.numpy as jnp
from jax import lax
from jax.experimental import pallas as pl
from jax.experimental.pallas import tpu as pltpu
from jax.sharding import PartitionSpec as P

F32 = jnp.float32
BF16 = jnp.bfloat16
VMEM_SPARE = 4 * 1024 * 1024
LANDINGS = 4
GATHER_BYTES = 16 * 1024 * 1024


def owner_tables(req_owner, req_slot, own_index, peer_count, slot_count, request_count):
    owners_all = req_owner[:, 0].reshape(peer_count, request_count)
    slots_all = req_slot.reshape(peer_count, request_count)
    mine = owners_all == own_index
    ranks = jnp.cumsum(mine.astype(jnp.int32), axis=1) - 1
    slot_ids = jnp.arange(slot_count, dtype=jnp.int32)
    chosen = mine[:, None, :] & (ranks[:, None, :] == slot_ids[None, :, None])
    send_index = jnp.sum(jnp.where(chosen, slots_all[:, None, :], 0), axis=2).reshape(-1)
    own_owners = lax.dynamic_slice_in_dim(req_owner[:, 0], own_index * request_count, request_count)
    request_ids = jnp.arange(request_count, dtype=jnp.int32)
    earlier = (own_owners[:, None] == own_owners[None, :]) & (
        request_ids[None, :] < request_ids[:, None]
    )
    own_rank = jnp.sum(earlier.astype(jnp.int32), axis=1)
    receive_index = own_owners * slot_count + own_rank
    return (send_index, receive_index)


class Rows:
    def __init__(self, tab, stride, first):
        self.tab, self.stride, self.first = tab, stride, first

    def __getitem__(self, at):
        return self.tab[0, at[0] * self.stride + self.first + at[1]]


def with_terms(kernel, terms, groups, scale):
    def run(tab, *rest):
        tl, tf, tr = (Rows(tab, groups * terms, i * terms) for i in (0, 1, groups - 1))
        kernel(terms, scale, tl, tr, tf, *rest)

    return run


def dot(a, b):
    return jnp.dot(a, b, preferred_element_type=F32)


def dot_rt(a, b):
    return lax.dot_general(a, b, (((1,), (1,)), ((), ())), preferred_element_type=F32)


def forward_sums(left, right, tl, tr, b, terms):
    lhs = jnp.concatenate([left[tl[b, t]] for t in range(terms)], axis=1)
    rhs = jnp.concatenate([right[tr[b, t]] for t in range(terms)], axis=0)
    return dot(lhs, rhs)


def left_adjoint(cots, right, tl, tr, acc, terms):
    acc[...] = jnp.zeros_like(acc)

    @pl.loop(0, cots.shape[0], unroll=8)
    def _(b):
        rhs = jnp.concatenate([right[tr[b, t]] for t in range(terms)], axis=0)
        piece = dot_rt(cots[b], rhs)
        width = cots.shape[2]
        for t in range(terms):
            acc[tl[b, t]] += piece[:, t * width:(t + 1) * width]


def gather_kernel(index, blocks, out):
    @pl.loop(0, out.shape[0], unroll=4)
    def _(s):
        out[s] = blocks[index[s]]


def square_phase(terms, scale, tl, tr, tf, dens, right, square):
    @pl.loop(0, dens.shape[0], unroll=16)
    def _(b):
        square[b] = (scale * forward_sums(dens, right, tl, tr, b, terms)).astype(BF16)


def fresh_phase(terms, scale, tl, tr, tf, square, right, fresh):
    @pl.loop(0, square.shape[0], unroll=16)
    def _(b):
        cube = scale * forward_sums(square, right, tl, tr, b, terms)
        fresh[b] = (3.0 * square[b].astype(F32) - 2.0 * cube).astype(BF16)


def forward_kernel(terms, scale, tl, tr, tf, index, dens, right, fresh, square, out):
    square_phase(terms, scale, tl, tr, tf, dens, right, square)
    fresh_phase(terms, scale, tl, tr, tf, square, right, fresh)
    gather_kernel(index, fresh, out)


def turn(dens, square, both):
    @pl.loop(0, dens.shape[0], unroll=8)
    def _(b):
        both[b] = jnp.concatenate([square[b].T, dens[b].T], axis=1)


def cot_phase(terms, scale, tl, tr, tf, row, blk, dens, right, cot, sqcot, sendback, acc, cube, both, racc, counts):
    blocks, width = dens.shape[0], dens.shape[2]

    @pl.loop(0, blocks, unroll=4)
    def _(b):
        cube[b] = (-2.0 * cot[b].astype(F32)).astype(BF16)

    left_adjoint(cube, right, tl, tr, acc, terms)

    @pl.loop(0, blocks, unroll=4)
    def _(b):
        sqcot[b] = (3.0 * cot[b].astype(F32) + scale * acc[b]).astype(BF16)

    racc[...] = jnp.zeros_like(racc)

    @pl.loop(0, blocks, unroll=8)
    def _(b):
        lhs = jnp.concatenate([both[tl[b, t]] for t in range(terms)], axis=0)
        rhs = jnp.concatenate([cube[b], sqcot[b]], axis=0)
        piece = dot(lhs, rhs)
        for t in range(terms):
            racc[tf[b, t]] += piece[t * width:(t + 1) * width]

    @pl.loop(0, sendback.shape[0], unroll=4)
    def _(s):
        sendback[s] = jnp.zeros(sendback.shape[1:], BF16)

    peers, requests = counts.shape[0], racc.shape[0]

    @pl.loop(0, peers)
    def _(p):
        counts[p] = 0

    @pl.loop(0, requests, unroll=4)
    def _(q):
        owner = blk[row[0] * requests + q] // blocks
        rank = counts[owner]
        counts[owner] = rank + 1
        slot = owner * (sendback.shape[0] // peers) + rank
        sendback[slot] = (scale * racc[q]).astype(BF16)


def reverse_kernel(terms, scale, tl, tr, tf, row, blk, dens, right, cot, square, sqcot, sendback, acc, cube, both, racc, counts):
    square_phase(terms, scale, tl, tr, tf, dens, right, square)
    turn(dens, square, both)
    cot_phase(terms, scale, tl, tr, tf, row, blk, dens, right, cot, sqcot, sendback, acc, cube, both, racc, counts)


def collect(index, returned, landing, sems, grad, before):
    size = returned.shape[0] // LANDINGS

    def fetch(i):
        span = pl.ds(i * size, size)
        return pltpu.make_async_copy(returned.at[span], landing.at[span], sems.at[i])

    for i in range(LANDINGS):
        fetch(i).start()
    before()
    for i in range(LANDINGS):
        fetch(i).wait()

        @pl.loop(0, size, unroll=8)
        def _(s):
            grad[index[i * size + s]] += landing[i * size + s].astype(F32)


def chained_kernel(terms, scale, tl, tr, tf, row, blk, index, dens, square, right, local, returned, sqcot, sendback, acc, cube, both, racc, counts, cot, landing, sems):
    def before():
        acc[...] = local[...]
        turn(dens, square, both)

    collect(index, returned, landing, sems, acc, before)
    cot[...] = acc[...].astype(BF16)
    cot_phase(terms, scale, tl, tr, tf, row, blk, dens, right, cot, sqcot, sendback, acc, cube, both, racc, counts)


def local_kernel(terms, scale, tl, tr, tf, sqcot, right, grad):
    left_adjoint(sqcot, right, tl, tr, grad, terms)
    grad[...] = scale * grad[...]


def final_kernel(index, local, returned, grad, landing, sems):
    def before():
        grad[...] = local[...]

    collect(index, returned, landing, sems, grad, before)


def spread_kernel(nz, ny, nc, parts, own, own_tab, spread, tabs, send_sem, recv_sem, own_sem):
    me = lax.axis_index("row")
    core, y, z = me % nc, (me // nc) % ny, me // (nc * ny)
    count = own.shape[0]
    size = count // parts
    UP, DOWN, ACROSS, TWIN = 0, 1, 2, 3
    steps = {UP: nc * ny, DOWN: -nc * ny}

    def target(way):
        if way == ACROSS:
            return (z * ny + (ny - 1 - y)) * nc + core
        if way == TWIN:
            return (z * ny + y) * nc + (nc - 1 - core)
        return me + steps[way]

    def exists(way):
        return {UP: z + 1 < nz, DOWN: z > 0}[way]

    barrier = pltpu.get_barrier_semaphore()

    def greet(way):
        pl.semaphore_signal(barrier, inc=1, device_id={"row": target(way)}, device_id_type=pl.DeviceIdType.MESH)

    for way in (UP, DOWN):
        pl.when(exists(way))(functools.partial(greet, way))
    for way in (ACROSS, TWIN):
        greet(way)
    pl.semaphore_wait(barrier, 2 + (z + 1 < nz).astype(jnp.int32) + (z > 0).astype(jnp.int32))

    TAB = parts

    def place_of(origin, s):
        if s is TAB:
            return tabs.at[origin]
        return spread.at[pl.ds(origin * count + s * size, size)]

    def copy(way, zz, yy, s, from_own=False):
        origin = (zz * ny + yy) * nc + core
        place = source = place_of(origin, s)
        if from_own:
            source = own_tab if s is TAB else own.at[pl.ds(s * size, size)]
        return pltpu.make_async_remote_copy(
            src_ref=source, dst_ref=place,
            send_sem=send_sem.at[way, zz * ny + yy, s], recv_sem=recv_sem.at[origin, s],
            device_id={"row": target(way)}, device_id_type=pl.DeviceIdType.MESH)

    def arrived(zz, yy, s, plane):
        origin = (zz * ny + yy) * nc + plane
        place = place_of(origin, s)
        pltpu.make_async_remote_copy(
            src_ref=place, dst_ref=place,
            send_sem=send_sem.at[TWIN, 0, 0], recv_sem=recv_sem.at[origin, s],
            device_id={"row": target(TWIN)}, device_id_type=pl.DeviceIdType.MESH).wait_recv()

    def maybe(way, act):
        pl.when(exists(way))(act)

    kept = pltpu.make_async_copy(own, spread.at[pl.ds(me * count, count)], own_sem.at[0])
    kept.start()
    kept_tab = pltpu.make_async_copy(own_tab, tabs.at[me], own_sem.at[1])
    kept_tab.start()

    def begin(s):
        maybe(UP, lambda: copy(UP, z, y, s, True).start())
        maybe(DOWN, lambda: copy(DOWN, z, y, s, True).start())
        copy(ACROSS, z, y, s, True).start()
        copy(TWIN, z, y, s, True).start()

    begin(TAB)
    pl.loop(0, parts)(begin)

    def along(d, s, yy, cross):
        for way, zz, there in ((UP, z - d, z >= d), (DOWN, z + d, z + d < nz)):
            @pl.when(there)
            def _(way=way, zz=zz):
                arrived(zz, yy, s, core)
                maybe(way, lambda: copy(way, zz, yy, s).start())
                if cross:
                    copy(ACROSS, zz, yy, s).start()
                copy(TWIN, zz, yy, s).start()

    other = ny - 1 - y
    arrived(z, other, 0, core)
    maybe(UP, lambda: copy(UP, z, other, 0).start())
    maybe(DOWN, lambda: copy(DOWN, z, other, 0).start())
    copy(TWIN, z, other, 0).start()

    def crossed(d, s):
        if d == 0:
            arrived(z, other, s, core)
            copy(TWIN, z, other, s).start()
        else:
            for zz, there in ((z - d, z >= d), (z + d, z + d < nz)):
                @pl.when(there)
                def _(zz=zz):
                    arrived(zz, other, s, core)
                    copy(TWIN, zz, other, s).start()

    def drain(d):
        crossed(d, TAB)
        pl.loop(1, parts)(functools.partial(crossed, d))

    for d in range(1, nz):
        along(d, 0, y, False)
        along(d, TAB, y, True)

        @pl.loop(1, parts)
        def _(s):
            along(d, s, y, True)

        along(d, 0, other, False)
        if d == 1:
            drain(0)

    for d in range(1, nz):
        drain(d)

    kept.wait()
    kept_tab.wait()

    @pl.loop(0, nz * ny)
    def _(i):
        arrived(i // ny, i % ny, TAB, nc - 1 - core)

        @pl.loop(0, parts)
        def _(s):
            arrived(i // ny, i % ny, s, nc - 1 - core)

    def sent(way, zz, yy, s):
        copy(way, zz, yy, s).wait_send()

    def finish(zz, s, first):
        for yy in range(ny):
            sent(TWIN, zz, yy, s)

        @pl.when(jnp.logical_or(jnp.logical_not(first), zz == z))
        def _():
            sent(ACROSS, zz, y, s)

        @pl.when((zz <= z) & (z + 1 < nz))
        def _():
            sent(UP, zz, y, s)

        @pl.when((zz >= z) & (z > 0))
        def _():
            sent(DOWN, zz, y, s)

        if s is not TAB:
            @pl.when(first & (zz <= z) & (z + 1 < nz))
            def _():
                sent(UP, zz, other, s)

            @pl.when(first & (zz >= z) & (z > 0))
            def _():
                sent(DOWN, zz, other, s)

    @pl.loop(0, nz)
    def _(zz):
        finish(zz, TAB, False)

        @pl.loop(0, parts)
        def _(s):
            finish(zz, s, s == 0)


def spread_all(own, own_tab, peers):
    nc, ny = 2, 2
    nz, parts = peers // (nc * ny), 8
    count, width = own.shape[0], own.shape[1]
    return pl.pallas_call(
        functools.partial(spread_kernel, nz, ny, nc, parts),
        out_shape=[
            jax.ShapeDtypeStruct((peers * count, width, width), own.dtype),
            jax.ShapeDtypeStruct((peers,) + own_tab.shape, own_tab.dtype),
        ],
        in_specs=[pl.BlockSpec(memory_space=pl.ANY)] * 2,
        out_specs=[pl.BlockSpec(memory_space=pl.ANY)] * 2,
        scratch_shapes=[
            pltpu.SemaphoreType.DMA((4, nz * ny, parts + 1)),
            pltpu.SemaphoreType.DMA((peers, parts + 1)),
            pltpu.SemaphoreType.DMA((2,)),
        ],
        compiler_params=pltpu.CompilerParams(collective_id=0, has_side_effects=True),
    )(own, own_tab)


def rebuild_kernel(terms, scale, tl, tr, tf, row, blk, tabs, whole, cot, fresh, square, right0, right1, square2, sqcot, sendback, acc, cube, both, racc, counts, parts):
    count, requests = fresh.shape[0], right0.shape[0]
    me = row[0]

    def term_ids(b):
        group, at = b // count, (b % count) * 2 * terms
        lefts = [group * count + tabs[group, 0, at + t] for t in range(terms)]
        rights = [blk[group * requests + tabs[group, 0, at + terms + t]] for t in range(terms)]
        return lefts, rights

    def product(left, lefts, rights):
        lhs = jnp.concatenate([left[i] for i in lefts], axis=1)
        rhs = jnp.concatenate([whole[i] for i in rights], axis=0)
        return scale * dot(lhs, rhs)

    @pl.loop(0, requests, unroll=4)
    def _(q):
        b = blk[me * requests + q]
        right0[q] = whole[b]
        lefts, _ = term_ids(b)
        for t, i in enumerate(lefts + [b]):
            parts[q * (terms + 1) + t] = product(whole, *term_ids(i)).astype(BF16)

    @pl.loop(0, requests, unroll=8)
    def _(q):
        _, rights = term_ids(blk[me * requests + q])
        at = q * (terms + 1)
        cubed = product(parts, [at + t for t in range(terms)], rights)
        right1[q] = (3.0 * parts[at + terms].astype(F32) - 2.0 * cubed).astype(BF16)

    square_phase(terms, scale, tl, tr, tf, whole.at[pl.ds(me * count, count)], right0, square)
    fresh_phase(terms, scale, tl, tr, tf, square, right0, fresh)
    reverse_kernel(terms, scale, tl, tr, tf, row, blk, fresh, right1, cot, square2, sqcot, sendback, acc, cube, both, racc, counts)


def call(kernel, prefetch, arrays, outs, scratch=(), flops=0, left_out=0):
    whole = pl.BlockSpec(memory_space=pltpu.VMEM)
    smem = pl.BlockSpec(memory_space=pltpu.SMEM)
    moved = sum(a.size * a.dtype.itemsize for a in arrays)
    held = [*arrays[:len(arrays) - left_out], *outs]
    held += [s for s in scratch if getattr(s, "memory_space", None) == pltpu.VMEM]
    room = sum(math.prod(a.shape) * jnp.dtype(a.dtype).itemsize for a in held) + VMEM_SPARE
    return pl.pallas_call(
        kernel,
        out_shape=outs,
        in_specs=[smem] * len(prefetch) + [whole] * (len(arrays) - left_out) + [pl.BlockSpec(memory_space=pl.ANY)] * left_out,
        out_specs=[whole] * len(outs),
        scratch_shapes=list(scratch),
        cost_estimate=pl.CostEstimate(flops=flops, bytes_accessed=moved, transcendentals=0),
        compiler_params=pltpu.CompilerParams(vmem_limit_bytes=room),
    )(*prefetch, *arrays)


def body(density_guess, cotangent, term_left, term_fetch, req_owner, req_slot):
    peer_count = lax.axis_size("row")
    own_index = lax.axis_index("row")
    request_count = req_owner.shape[0] // peer_count
    slot_count = max(2, 2 * request_count // peer_count)
    blocks, width = density_guess.shape[0], density_guess.shape[1]
    terms = term_left.shape[1]
    scale = float(width * terms) ** (-0.5)
    slots = peer_count * slot_count
    row = own_index.reshape(1)
    named = req_owner[:, 0] * blocks + req_slot

    def shape(n, dtype):
        return jax.ShapeDtypeStruct((n, width, width), dtype)

    def exchange(x):
        return lax.all_to_all(x, "row", split_axis=0, concat_axis=0, tiled=True)

    work = 2 * blocks * terms * width ** 3
    common = [
        pltpu.VMEM((blocks, width, width), F32),
        pltpu.VMEM((blocks, width, width), BF16),
        pltpu.VMEM((blocks, width, 2 * width), BF16),
        pltpu.VMEM((request_count, width, width), F32),
        pltpu.SMEM((peer_count,), jnp.int32),
    ]

    landing = [pltpu.VMEM((slots, width, width), BF16), pltpu.SemaphoreType.DMA((LANDINGS,))]

    def packed(*columns):
        tab = jnp.concatenate(columns, axis=1).reshape(1, -1)
        return jnp.broadcast_to(tab, (8, tab.shape[1]))

    def routes(owner, slot):
        return owner_tables(owner, slot, own_index, peer_count, slot_count, request_count)

    if peer_count * blocks * width * width * 2 <= GATHER_BYTES and peer_count % 4 == 0:
        tab, groups = packed(term_left, term_fetch), 2
        whole, tabs = spread_all(density_guess, tab, peer_count)
        first, square1, right0, right1, square2, sqcot2, back2 = call(
            with_terms(rebuild_kernel, terms, groups, scale),
            [tab, row, named, tabs], [whole, cotangent],
            [shape(blocks, BF16), shape(blocks, BF16), shape(request_count, BF16), shape(request_count, BF16),
             shape(blocks, BF16), shape(blocks, BF16), shape(slots, BF16)],
            common + [pltpu.VMEM((request_count * (terms + 1), width, width), BF16)], flops=(peer_count + 6) * work)
        owner, slot, back2 = lax.optimization_barrier((req_owner, req_slot, back2))
        send_index, _ = routes(owner, slot)
    else:
        send_index, receive_index = routes(req_owner, req_slot)
        tab, groups = packed(term_left, term_fetch, receive_index[term_fetch]), 3
        (out0,) = call(gather_kernel, [send_index], [density_guess], [shape(slots, BF16)])
        right0 = exchange(out0)
        first, square1, out1 = call(
            with_terms(forward_kernel, terms, groups, scale), [tab, send_index], [density_guess, right0],
            [shape(blocks, BF16), shape(blocks, BF16), shape(slots, BF16)], flops=2 * work)
        right1 = exchange(out1)
        square2, sqcot2, back2 = call(
            with_terms(reverse_kernel, terms, groups, scale), [tab, row, named],
            [first, right1, cotangent],
            [shape(blocks, BF16), shape(blocks, BF16), shape(slots, BF16)], common, flops=4 * work)
    returned2 = exchange(back2)
    (second,) = call(
        with_terms(fresh_phase, terms, groups, scale), [tab], [square2, right1], [shape(blocks, BF16)], flops=work)
    local = with_terms(local_kernel, terms, groups, scale)
    (local2,) = call(local, [tab], [sqcot2, right1], [shape(blocks, F32)], flops=work)
    sqcot1, back1 = call(
        with_terms(chained_kernel, terms, groups, scale), [tab, row, named, send_index],
        [density_guess, square1, right0, local2, returned2],
        [shape(blocks, BF16), shape(slots, BF16)],
        common + [pltpu.VMEM((blocks, width, width), BF16)] + landing, flops=3 * work, left_out=1)
    returned1 = exchange(back1)
    (local1,) = call(local, [tab], [sqcot1, right0], [shape(blocks, F32)], flops=work)
    (grad,) = call(final_kernel, [send_index], [local1, returned1], [shape(blocks, F32)], landing, left_out=1)
    return (second, grad)


def solution(mesh):
    placed = (
        P(("groups", "row"), None, None),
        P(("groups", "row"), None, None),
        P(("groups", "row"), None),
        P(("groups", "row"), None),
        P("groups", None),
        P("groups"),
    )
    return jax.shard_map(
        body,
        mesh=mesh,
        in_specs=placed,
        out_specs=(P(("groups", "row"), None, None), P(("groups", "row"), None, None)),
        check_vma=False,
    )
```

```python
import functools
import math

import jax
import jax.numpy as jnp
from jax import lax
from jax.experimental import pallas as pl
from jax.experimental.pallas import tpu as pltpu
from jax.sharding import PartitionSpec as P

F32 = jnp.float32
BF16 = jnp.bfloat16
VMEM_LIMIT = 56 * 1024 * 1024
VMEM_SPARE = 4 * 1024 * 1024
LANDINGS = 4
GATHER_BYTES = 16 * 1024 * 1024


def owner_tables(req_owner, req_slot, own_index, peer_count, slot_count, request_count):
    owners_all = req_owner[:, 0].reshape(peer_count, request_count)
    slots_all = req_slot.reshape(peer_count, request_count)
    mine = owners_all == own_index
    ranks = jnp.cumsum(mine.astype(jnp.int32), axis=1) - 1
    slot_ids = jnp.arange(slot_count, dtype=jnp.int32)
    chosen = mine[:, None, :] & (ranks[:, None, :] == slot_ids[None, :, None])
    send_index = jnp.sum(jnp.where(chosen, slots_all[:, None, :], 0), axis=2).reshape(-1)
    own_owners = lax.dynamic_slice_in_dim(req_owner[:, 0], own_index * request_count, request_count)
    request_ids = jnp.arange(request_count, dtype=jnp.int32)
    earlier = (own_owners[:, None] == own_owners[None, :]) & (
        request_ids[None, :] < request_ids[:, None]
    )
    own_rank = jnp.sum(earlier.astype(jnp.int32), axis=1)
    receive_index = own_owners * slot_count + own_rank
    return (send_index, receive_index)


class Rows:
    def __init__(self, tab, stride, first):
        self.tab, self.stride, self.first = tab, stride, first

    def __getitem__(self, at):
        return self.tab[0, at[0] * self.stride + self.first + at[1]]


def with_terms(kernel, terms, groups, scale):
    def run(tab, *rest):
        tl, tf, tr = (Rows(tab, groups * terms, i * terms) for i in (0, 1, groups - 1))
        kernel(terms, scale, tl, tr, tf, *rest)

    return run


def dot(a, b):
    return jnp.dot(a, b, preferred_element_type=F32)


def dot_rt(a, b):
    return lax.dot_general(a, b, (((1,), (1,)), ((), ())), preferred_element_type=F32)


def forward_sums(left, right, tl, tr, b, terms):
    lhs = jnp.concatenate([left[tl[b, t]] for t in range(terms)], axis=1)
    rhs = jnp.concatenate([right[tr[b, t]] for t in range(terms)], axis=0)
    return dot(lhs, rhs)


def left_adjoint(cots, right, tl, tr, acc, terms):
    acc[...] = jnp.zeros_like(acc)

    @pl.loop(0, cots.shape[0], unroll=8)
    def _(b):
        rhs = jnp.concatenate([right[tr[b, t]] for t in range(terms)], axis=0)
        piece = dot_rt(cots[b], rhs)
        width = cots.shape[2]
        for t in range(terms):
            acc[tl[b, t]] += piece[:, t * width:(t + 1) * width]


def gather_kernel(index, blocks, out):
    @pl.loop(0, out.shape[0], unroll=4)
    def _(s):
        out[s] = blocks[index[s]]


def square_phase(terms, scale, tl, tr, tf, dens, right, square):
    @pl.loop(0, dens.shape[0], unroll=16)
    def _(b):
        square[b] = (scale * forward_sums(dens, right, tl, tr, b, terms)).astype(BF16)


def fresh_phase(terms, scale, tl, tr, tf, square, right, fresh):
    @pl.loop(0, square.shape[0], unroll=16)
    def _(b):
        cube = scale * forward_sums(square, right, tl, tr, b, terms)
        fresh[b] = (3.0 * square[b].astype(F32) - 2.0 * cube).astype(BF16)


def forward_kernel(terms, scale, tl, tr, tf, index, dens, right, fresh, square, out):
    square_phase(terms, scale, tl, tr, tf, dens, right, square)
    fresh_phase(terms, scale, tl, tr, tf, square, right, fresh)
    gather_kernel(index, fresh, out)


def turn(dens, square, both):
    @pl.loop(0, dens.shape[0], unroll=8)
    def _(b):
        both[b] = jnp.concatenate([square[b].T, dens[b].T], axis=1)


def cot_phase(terms, scale, tl, tr, tf, row, blk, dens, right, cot, sqcot, sendback, acc, cube, both, racc, counts):
    blocks, width = dens.shape[0], dens.shape[2]

    @pl.loop(0, blocks, unroll=4)
    def _(b):
        cube[b] = (-2.0 * cot[b].astype(F32)).astype(BF16)

    left_adjoint(cube, right, tl, tr, acc, terms)

    @pl.loop(0, blocks, unroll=4)
    def _(b):
        sqcot[b] = (3.0 * cot[b].astype(F32) + scale * acc[b]).astype(BF16)

    racc[...] = jnp.zeros_like(racc)

    @pl.loop(0, blocks, unroll=8)
    def _(b):
        lhs = jnp.concatenate([both[tl[b, t]] for t in range(terms)], axis=0)
        rhs = jnp.concatenate([cube[b], sqcot[b]], axis=0)
        piece = dot(lhs, rhs)
        for t in range(terms):
            racc[tf[b, t]] += piece[t * width:(t + 1) * width]

    @pl.loop(0, sendback.shape[0], unroll=4)
    def _(s):
        sendback[s] = jnp.zeros(sendback.shape[1:], BF16)

    peers, requests = counts.shape[0], racc.shape[0]

    @pl.loop(0, peers)
    def _(p):
        counts[p] = 0

    @pl.loop(0, requests, unroll=4)
    def _(q):
        owner = blk[row[0] * requests + q] // blocks
        rank = counts[owner]
        counts[owner] = rank + 1
        slot = owner * (sendback.shape[0] // peers) + rank
        sendback[slot] = (scale * racc[q]).astype(BF16)


def reverse_kernel(terms, scale, tl, tr, tf, row, blk, dens, right, cot, square, sqcot, sendback, acc, cube, both, racc, counts):
    square_phase(terms, scale, tl, tr, tf, dens, right, square)
    turn(dens, square, both)
    cot_phase(terms, scale, tl, tr, tf, row, blk, dens, right, cot, sqcot, sendback, acc, cube, both, racc, counts)


def collect(index, returned, landing, sems, grad, before):
    size = returned.shape[0] // LANDINGS

    def fetch(i):
        span = pl.ds(i * size, size)
        return pltpu.make_async_copy(returned.at[span], landing.at[span], sems.at[i])

    for i in range(LANDINGS):
        fetch(i).start()
    before()
    for i in range(LANDINGS):
        fetch(i).wait()

        @pl.loop(0, size, unroll=8)
        def _(s):
            grad[index[i * size + s]] += landing[i * size + s].astype(F32)


def chained_kernel(terms, scale, tl, tr, tf, row, blk, index, dens, square, right, local, returned, sqcot, sendback, acc, cube, both, racc, counts, cot, landing, sems):
    def before():
        acc[...] = local[...]
        turn(dens, square, both)

    collect(index, returned, landing, sems, acc, before)
    cot[...] = acc[...].astype(BF16)
    cot_phase(terms, scale, tl, tr, tf, row, blk, dens, right, cot, sqcot, sendback, acc, cube, both, racc, counts)


def local_kernel(terms, scale, tl, tr, tf, sqcot, right, grad):
    left_adjoint(sqcot, right, tl, tr, grad, terms)
    grad[...] = scale * grad[...]


def final_kernel(index, local, returned, grad, landing, sems):
    def before():
        grad[...] = local[...]

    collect(index, returned, landing, sems, grad, before)


def spread_kernel(nz, ny, nc, parts, own, own_tab, spread, tabs, send_sem, recv_sem, own_sem):
    me = lax.axis_index("row")
    core, y, z = me % nc, (me // nc) % ny, me // (nc * ny)
    count = own.shape[0]
    size = count // parts
    UP, DOWN, ACROSS, TWIN = 0, 1, 2, 3
    steps = {UP: nc * ny, DOWN: -nc * ny}

    def target(way):
        if way == ACROSS:
            return (z * ny + (ny - 1 - y)) * nc + core
        if way == TWIN:
            return (z * ny + y) * nc + (nc - 1 - core)
        return me + steps[way]

    def exists(way):
        return {UP: z + 1 < nz, DOWN: z > 0}[way]

    barrier = pltpu.get_barrier_semaphore()

    def greet(way):
        pl.semaphore_signal(barrier, inc=1, device_id={"row": target(way)}, device_id_type=pl.DeviceIdType.MESH)

    for way in (UP, DOWN):
        pl.when(exists(way))(functools.partial(greet, way))
    for way in (ACROSS, TWIN):
        greet(way)
    pl.semaphore_wait(barrier, 2 + (z + 1 < nz).astype(jnp.int32) + (z > 0).astype(jnp.int32))

    TAB = parts

    def place_of(origin, s):
        if s is TAB:
            return tabs.at[origin]
        return spread.at[pl.ds(origin * count + s * size, size)]

    def copy(way, zz, yy, s, from_own=False):
        origin = (zz * ny + yy) * nc + core
        place = source = place_of(origin, s)
        if from_own:
            source = own_tab if s is TAB else own.at[pl.ds(s * size, size)]
        return pltpu.make_async_remote_copy(
            src_ref=source, dst_ref=place,
            send_sem=send_sem.at[way, zz * ny + yy, s], recv_sem=recv_sem.at[origin, s],
            device_id={"row": target(way)}, device_id_type=pl.DeviceIdType.MESH)

    def arrived(zz, yy, s, plane):
        origin = (zz * ny + yy) * nc + plane
        place = place_of(origin, s)
        pltpu.make_async_remote_copy(
            src_ref=place, dst_ref=place,
            send_sem=send_sem.at[TWIN, 0, 0], recv_sem=recv_sem.at[origin, s],
            device_id={"row": target(TWIN)}, device_id_type=pl.DeviceIdType.MESH).wait_recv()

    def maybe(way, act):
        pl.when(exists(way))(act)

    kept = pltpu.make_async_copy(own, spread.at[pl.ds(me * count, count)], own_sem.at[0])
    kept.start()
    kept_tab = pltpu.make_async_copy(own_tab, tabs.at[me], own_sem.at[1])
    kept_tab.start()

    def begin(s):
        maybe(UP, lambda: copy(UP, z, y, s, True).start())
        maybe(DOWN, lambda: copy(DOWN, z, y, s, True).start())
        copy(ACROSS, z, y, s, True).start()
        copy(TWIN, z, y, s, True).start()

    begin(TAB)
    pl.loop(0, parts)(begin)

    def along(d, s, yy, cross):
        for way, zz, there in ((UP, z - d, z >= d), (DOWN, z + d, z + d < nz)):
            @pl.when(there)
            def _(way=way, zz=zz):
                arrived(zz, yy, s, core)
                maybe(way, lambda: copy(way, zz, yy, s).start())
                if cross:
                    copy(ACROSS, zz, yy, s).start()
                copy(TWIN, zz, yy, s).start()

    other = ny - 1 - y
    arrived(z, other, 0, core)
    maybe(UP, lambda: copy(UP, z, other, 0).start())
    maybe(DOWN, lambda: copy(DOWN, z, other, 0).start())
    copy(TWIN, z, other, 0).start()

    def crossed(d, s):
        if d == 0:
            arrived(z, other, s, core)
            copy(TWIN, z, other, s).start()
        else:
            for zz, there in ((z - d, z >= d), (z + d, z + d < nz)):
                @pl.when(there)
                def _(zz=zz):
                    arrived(zz, other, s, core)
                    copy(TWIN, zz, other, s).start()

    def drain(d):
        crossed(d, TAB)
        pl.loop(1, parts)(functools.partial(crossed, d))

    for d in range(1, nz):
        along(d, 0, y, False)
        along(d, TAB, y, True)

        @pl.loop(1, parts)
        def _(s):
            along(d, s, y, True)

        along(d, 0, other, False)
        if d == 1:
            drain(0)

    for d in range(1, nz):
        drain(d)

    kept.wait()
    kept_tab.wait()

    @pl.loop(0, nz * ny)
    def _(i):
        arrived(i // ny, i % ny, TAB, nc - 1 - core)

        @pl.loop(0, parts)
        def _(s):
            arrived(i // ny, i % ny, s, nc - 1 - core)

    def sent(way, zz, yy, s):
        copy(way, zz, yy, s).wait_send()

    def finish(zz, s, first):
        for yy in range(ny):
            sent(TWIN, zz, yy, s)

        @pl.when(jnp.logical_or(jnp.logical_not(first), zz == z))
        def _():
            sent(ACROSS, zz, y, s)

        @pl.when((zz <= z) & (z + 1 < nz))
        def _():
            sent(UP, zz, y, s)

        @pl.when((zz >= z) & (z > 0))
        def _():
            sent(DOWN, zz, y, s)

        if s is not TAB:
            @pl.when(first & (zz <= z) & (z + 1 < nz))
            def _():
                sent(UP, zz, other, s)

            @pl.when(first & (zz >= z) & (z > 0))
            def _():
                sent(DOWN, zz, other, s)

    @pl.loop(0, nz)
    def _(zz):
        finish(zz, TAB, False)

        @pl.loop(0, parts)
        def _(s):
            finish(zz, s, s == 0)


def spread_all(own, own_tab, peers):
    nc, ny = 2, 2
    nz, parts = peers // (nc * ny), 8
    count, width = own.shape[0], own.shape[1]
    return pl.pallas_call(
        functools.partial(spread_kernel, nz, ny, nc, parts),
        out_shape=[
            jax.ShapeDtypeStruct((peers * count, width, width), own.dtype),
            jax.ShapeDtypeStruct((peers,) + own_tab.shape, own_tab.dtype),
        ],
        in_specs=[pl.BlockSpec(memory_space=pl.ANY)] * 2,
        out_specs=[pl.BlockSpec(memory_space=pl.ANY)] * 2,
        scratch_shapes=[
            pltpu.SemaphoreType.DMA((4, nz * ny, parts + 1)),
            pltpu.SemaphoreType.DMA((peers, parts + 1)),
            pltpu.SemaphoreType.DMA((2,)),
        ],
        compiler_params=pltpu.CompilerParams(collective_id=0, has_side_effects=True),
    )(own, own_tab)


def rebuild_kernel(terms, scale, tl, tr, tf, row, blk, tabs, whole, cot, fresh, square, right0, right1, square2, sqcot, sendback, acc, cube, both, racc, counts, parts):
    count, requests = fresh.shape[0], right0.shape[0]
    me = row[0]

    def term_ids(b):
        group, at = b // count, (b % count) * 2 * terms
        lefts = [group * count + tabs[group, 0, at + t] for t in range(terms)]
        rights = [blk[group * requests + tabs[group, 0, at + terms + t]] for t in range(terms)]
        return lefts, rights

    def product(left, lefts, rights):
        lhs = jnp.concatenate([left[i] for i in lefts], axis=1)
        rhs = jnp.concatenate([whole[i] for i in rights], axis=0)
        return scale * dot(lhs, rhs)

    @pl.loop(0, requests, unroll=4)
    def _(q):
        b = blk[me * requests + q]
        right0[q] = whole[b]
        lefts, _ = term_ids(b)
        for t, i in enumerate(lefts + [b]):
            parts[q * (terms + 1) + t] = product(whole, *term_ids(i)).astype(BF16)

    @pl.loop(0, requests, unroll=8)
    def _(q):
        _, rights = term_ids(blk[me * requests + q])
        at = q * (terms + 1)
        cubed = product(parts, [at + t for t in range(terms)], rights)
        right1[q] = (3.0 * parts[at + terms].astype(F32) - 2.0 * cubed).astype(BF16)

    square_phase(terms, scale, tl, tr, tf, whole.at[pl.ds(me * count, count)], right0, square)
    fresh_phase(terms, scale, tl, tr, tf, square, right0, fresh)
    reverse_kernel(terms, scale, tl, tr, tf, row, blk, fresh, right1, cot, square2, sqcot, sendback, acc, cube, both, racc, counts)


def call(kernel, prefetch, arrays, outs, scratch=(), flops=0, left_out=0, tight=False):
    whole = pl.BlockSpec(memory_space=pltpu.VMEM)
    smem = pl.BlockSpec(memory_space=pltpu.SMEM)
    moved = sum(a.size * a.dtype.itemsize for a in arrays)
    held = [*arrays[:len(arrays) - left_out], *outs]
    held += [s for s in scratch if getattr(s, "memory_space", None) == pltpu.VMEM]
    room = sum(math.prod(a.shape) * jnp.dtype(a.dtype).itemsize for a in held) + VMEM_SPARE
    return pl.pallas_call(
        kernel,
        out_shape=outs,
        in_specs=[smem] * len(prefetch) + [whole] * (len(arrays) - left_out) + [pl.BlockSpec(memory_space=pl.ANY)] * left_out,
        out_specs=[whole] * len(outs),
        scratch_shapes=list(scratch),
        cost_estimate=pl.CostEstimate(flops=flops, bytes_accessed=moved, transcendentals=0),
        compiler_params=pltpu.CompilerParams(vmem_limit_bytes=room if tight else VMEM_LIMIT),
    )(*prefetch, *arrays)


def body(density_guess, cotangent, term_left, term_fetch, req_owner, req_slot):
    peer_count = lax.axis_size("row")
    own_index = lax.axis_index("row")
    request_count = req_owner.shape[0] // peer_count
    slot_count = max(2, 2 * request_count // peer_count)
    blocks, width = density_guess.shape[0], density_guess.shape[1]
    terms = term_left.shape[1]
    scale = float(width * terms) ** (-0.5)
    slots = peer_count * slot_count
    row = own_index.reshape(1)
    named = req_owner[:, 0] * blocks + req_slot

    def shape(n, dtype):
        return jax.ShapeDtypeStruct((n, width, width), dtype)

    def exchange(x):
        return lax.all_to_all(x, "row", split_axis=0, concat_axis=0, tiled=True)

    work = 2 * blocks * terms * width ** 3
    common = [
        pltpu.VMEM((blocks, width, width), F32),
        pltpu.VMEM((blocks, width, width), BF16),
        pltpu.VMEM((blocks, width, 2 * width), BF16),
        pltpu.VMEM((request_count, width, width), F32),
        pltpu.SMEM((peer_count,), jnp.int32),
    ]

    landing = [pltpu.VMEM((slots, width, width), BF16), pltpu.SemaphoreType.DMA((LANDINGS,))]

    def packed(*columns):
        tab = jnp.concatenate(columns, axis=1).reshape(1, -1)
        return jnp.broadcast_to(tab, (8, tab.shape[1]))

    def routes(owner, slot):
        return owner_tables(owner, slot, own_index, peer_count, slot_count, request_count)

    if peer_count * blocks * width * width * 2 <= GATHER_BYTES and peer_count % 4 == 0:
        tab, groups = packed(term_left, term_fetch), 2
        whole, tabs = spread_all(density_guess, tab, peer_count)
        first, square1, right0, right1, square2, sqcot2, back2 = call(
            with_terms(rebuild_kernel, terms, groups, scale),
            [tab, row, named, tabs], [whole, cotangent],
            [shape(blocks, BF16), shape(blocks, BF16), shape(request_count, BF16), shape(request_count, BF16),
             shape(blocks, BF16), shape(blocks, BF16), shape(slots, BF16)],
            common + [pltpu.VMEM((request_count * (terms + 1), width, width), BF16)], flops=(peer_count + 6) * work)
        owner, slot, back2 = lax.optimization_barrier((req_owner, req_slot, back2))
        send_index, _ = routes(owner, slot)
    else:
        send_index, receive_index = routes(req_owner, req_slot)
        tab, groups = packed(term_left, term_fetch, receive_index[term_fetch]), 3
        (out0,) = call(gather_kernel, [send_index], [density_guess], [shape(slots, BF16)])
        right0 = exchange(out0)
        first, square1, out1 = call(
            with_terms(forward_kernel, terms, groups, scale), [tab, send_index], [density_guess, right0],
            [shape(blocks, BF16), shape(blocks, BF16), shape(slots, BF16)], flops=2 * work)
        right1 = exchange(out1)
        square2, sqcot2, back2 = call(
            with_terms(reverse_kernel, terms, groups, scale), [tab, row, named],
            [first, right1, cotangent],
            [shape(blocks, BF16), shape(blocks, BF16), shape(slots, BF16)], common, flops=4 * work)
    returned2 = exchange(back2)
    (second,) = call(
        with_terms(fresh_phase, terms, groups, scale), [tab], [square2, right1], [shape(blocks, BF16)], flops=work)
    local = with_terms(local_kernel, terms, groups, scale)
    (local2,) = call(local, [tab], [sqcot2, right1], [shape(blocks, F32)], flops=work)
    sqcot1, back1 = call(
        with_terms(chained_kernel, terms, groups, scale), [tab, row, named, send_index],
        [density_guess, square1, right0, local2, returned2],
        [shape(blocks, BF16), shape(slots, BF16)],
        common + [pltpu.VMEM((blocks, width, width), BF16)] + landing, flops=3 * work, left_out=1)
    returned1 = exchange(back1)
    (local1,) = call(local, [tab], [sqcot1, right0], [shape(blocks, F32)], flops=work)
    (grad,) = call(final_kernel, [send_index], [local1, returned1], [shape(blocks, F32)], landing, left_out=1, tight=True)
    return (second, grad)


def solution(mesh):
    placed = (
        P(("groups", "row"), None, None),
        P(("groups", "row"), None, None),
        P(("groups", "row"), None),
        P(("groups", "row"), None),
        P("groups", None),
        P("groups"),
    )
    return jax.shard_map(
        body,
        mesh=mesh,
        in_specs=placed,
        out_specs=(P(("groups", "row"), None, None), P(("groups", "row"), None, None)),
        check_vma=False,
    )
```

```python
import functools
import math

import jax
import jax.numpy as jnp
from jax import lax
from jax.experimental import pallas as pl
from jax.experimental.pallas import tpu as pltpu
from jax.sharding import PartitionSpec as P

F32 = jnp.float32
BF16 = jnp.bfloat16
VMEM_LIMIT = 56 * 1024 * 1024
VMEM_SPARE = 4 * 1024 * 1024
LANDINGS = 4
GATHER_BYTES = 16 * 1024 * 1024


def owner_tables(req_owner, req_slot, own_index, peer_count, slot_count, request_count):
    owners_all = req_owner[:, 0].reshape(peer_count, request_count)
    slots_all = req_slot.reshape(peer_count, request_count)
    mine = owners_all == own_index
    ranks = jnp.cumsum(mine.astype(jnp.int32), axis=1) - 1
    slot_ids = jnp.arange(slot_count, dtype=jnp.int32)
    chosen = mine[:, None, :] & (ranks[:, None, :] == slot_ids[None, :, None])
    send_index = jnp.sum(jnp.where(chosen, slots_all[:, None, :], 0), axis=2).reshape(-1)
    own_owners = lax.dynamic_slice_in_dim(req_owner[:, 0], own_index * request_count, request_count)
    request_ids = jnp.arange(request_count, dtype=jnp.int32)
    earlier = (own_owners[:, None] == own_owners[None, :]) & (
        request_ids[None, :] < request_ids[:, None]
    )
    own_rank = jnp.sum(earlier.astype(jnp.int32), axis=1)
    receive_index = own_owners * slot_count + own_rank
    return (send_index, receive_index)


class Rows:
    def __init__(self, tab, stride, first):
        self.tab, self.stride, self.first = tab, stride, first

    def __getitem__(self, at):
        return self.tab[0, at[0] * self.stride + self.first + at[1]]


def with_terms(kernel, terms, groups, scale):
    def run(tab, *rest):
        tl, tf, tr = (Rows(tab, groups * terms, i * terms) for i in (0, 1, groups - 1))
        kernel(terms, scale, tl, tr, tf, *rest)

    return run


def dot(a, b):
    return jnp.dot(a, b, preferred_element_type=F32)


def dot_rt(a, b):
    return lax.dot_general(a, b, (((1,), (1,)), ((), ())), preferred_element_type=F32)


def forward_sums(left, right, tl, tr, b, terms):
    lhs = jnp.concatenate([left[tl[b, t]] for t in range(terms)], axis=1)
    rhs = jnp.concatenate([right[tr[b, t]] for t in range(terms)], axis=0)
    return dot(lhs, rhs)


def left_adjoint(cots, right, tl, tr, acc, terms):
    acc[...] = jnp.zeros_like(acc)

    @pl.loop(0, cots.shape[0], unroll=8)
    def _(b):
        rhs = jnp.concatenate([right[tr[b, t]] for t in range(terms)], axis=0)
        piece = dot_rt(cots[b], rhs)
        width = cots.shape[2]
        for t in range(terms):
            acc[tl[b, t]] += piece[:, t * width:(t + 1) * width]


def gather_kernel(index, blocks, out):
    @pl.loop(0, out.shape[0], unroll=4)
    def _(s):
        out[s] = blocks[index[s]]


def square_phase(terms, scale, tl, tr, tf, dens, right, square):
    @pl.loop(0, dens.shape[0], unroll=16)
    def _(b):
        square[b] = (scale * forward_sums(dens, right, tl, tr, b, terms)).astype(BF16)


def fresh_phase(terms, scale, tl, tr, tf, square, right, fresh):
    @pl.loop(0, square.shape[0], unroll=16)
    def _(b):
        cube = scale * forward_sums(square, right, tl, tr, b, terms)
        fresh[b] = (3.0 * square[b].astype(F32) - 2.0 * cube).astype(BF16)


def forward_kernel(terms, scale, tl, tr, tf, index, dens, right, fresh, square, out):
    square_phase(terms, scale, tl, tr, tf, dens, right, square)
    fresh_phase(terms, scale, tl, tr, tf, square, right, fresh)
    gather_kernel(index, fresh, out)


def turn(dens, square, both):
    @pl.loop(0, dens.shape[0], unroll=8)
    def _(b):
        both[b] = jnp.concatenate([square[b].T, dens[b].T], axis=1)


def cot_phase(terms, scale, tl, tr, tf, row, blk, dens, right, cot, sqcot, sendback, acc, cube, both, racc, counts):
    blocks, width = dens.shape[0], dens.shape[2]

    @pl.loop(0, blocks, unroll=4)
    def _(b):
        cube[b] = (-2.0 * cot[b].astype(F32)).astype(BF16)

    left_adjoint(cube, right, tl, tr, acc, terms)

    @pl.loop(0, blocks, unroll=4)
    def _(b):
        sqcot[b] = (3.0 * cot[b].astype(F32) + scale * acc[b]).astype(BF16)

    racc[...] = jnp.zeros_like(racc)

    @pl.loop(0, blocks, unroll=8)
    def _(b):
        lhs = jnp.concatenate([both[tl[b, t]] for t in range(terms)], axis=0)
        rhs = jnp.concatenate([cube[b], sqcot[b]], axis=0)
        piece = dot(lhs, rhs)
        for t in range(terms):
            racc[tf[b, t]] += piece[t * width:(t + 1) * width]

    @pl.loop(0, sendback.shape[0], unroll=4)
    def _(s):
        sendback[s] = jnp.zeros(sendback.shape[1:], BF16)

    peers, requests = counts.shape[0], racc.shape[0]

    @pl.loop(0, peers)
    def _(p):
        counts[p] = 0

    @pl.loop(0, requests, unroll=4)
    def _(q):
        owner = blk[row[0] * requests + q] // blocks
        rank = counts[owner]
        counts[owner] = rank + 1
        slot = owner * (sendback.shape[0] // peers) + rank
        sendback[slot] = (scale * racc[q]).astype(BF16)


def reverse_kernel(terms, scale, tl, tr, tf, row, blk, dens, right, cot, square, sqcot, sendback, acc, cube, both, racc, counts):
    square_phase(terms, scale, tl, tr, tf, dens, right, square)
    turn(dens, square, both)
    cot_phase(terms, scale, tl, tr, tf, row, blk, dens, right, cot, sqcot, sendback, acc, cube, both, racc, counts)


def collect(index, returned, landing, sems, grad, before):
    size = returned.shape[0] // LANDINGS

    def fetch(i):
        span = pl.ds(i * size, size)
        return pltpu.make_async_copy(returned.at[span], landing.at[span], sems.at[i])

    for i in range(LANDINGS):
        fetch(i).start()
    before()
    for i in range(LANDINGS):
        fetch(i).wait()

        @pl.loop(0, size, unroll=8)
        def _(s):
            grad[index[i * size + s]] += landing[i * size + s].astype(F32)


def chained_kernel(terms, scale, tl, tr, tf, row, blk, index, dens, square, right, local, returned, sqcot, sendback, acc, cube, both, racc, counts, cot, landing, sems):
    def before():
        acc[...] = local[...]
        turn(dens, square, both)

    collect(index, returned, landing, sems, acc, before)
    cot[...] = acc[...].astype(BF16)
    cot_phase(terms, scale, tl, tr, tf, row, blk, dens, right, cot, sqcot, sendback, acc, cube, both, racc, counts)


def local_kernel(terms, scale, tl, tr, tf, sqcot, right, grad):
    left_adjoint(sqcot, right, tl, tr, grad, terms)
    grad[...] = scale * grad[...]


def final_kernel(index, local, returned, grad, landing, sems):
    def before():
        grad[...] = local[...]

    collect(index, returned, landing, sems, grad, before)


def spread_kernel(nz, ny, nc, parts, own, own_tab, spread, tabs, send_sem, recv_sem, own_sem):
    me = lax.axis_index("row")
    core, y, z = me % nc, (me // nc) % ny, me // (nc * ny)
    count = own.shape[0]
    size = count // parts
    UP, DOWN, ACROSS, TWIN = 0, 1, 2, 3
    steps = {UP: nc * ny, DOWN: -nc * ny}

    def target(way):
        if way == ACROSS:
            return (z * ny + (ny - 1 - y)) * nc + core
        if way == TWIN:
            return (z * ny + y) * nc + (nc - 1 - core)
        return me + steps[way]

    def exists(way):
        return {UP: z + 1 < nz, DOWN: z > 0}[way]

    barrier = pltpu.get_barrier_semaphore()

    def greet(way):
        pl.semaphore_signal(barrier, inc=1, device_id={"row": target(way)}, device_id_type=pl.DeviceIdType.MESH)

    for way in (UP, DOWN):
        pl.when(exists(way))(functools.partial(greet, way))
    for way in (ACROSS, TWIN):
        greet(way)
    pl.semaphore_wait(barrier, 2 + (z + 1 < nz).astype(jnp.int32) + (z > 0).astype(jnp.int32))

    TAB = parts

    def place_of(origin, s):
        if s is TAB:
            return tabs.at[origin]
        return spread.at[pl.ds(origin * count + s * size, size)]

    def copy(way, zz, yy, s, from_own=False):
        origin = (zz * ny + yy) * nc + core
        place = source = place_of(origin, s)
        if from_own:
            source = own_tab if s is TAB else own.at[pl.ds(s * size, size)]
        return pltpu.make_async_remote_copy(
            src_ref=source, dst_ref=place,
            send_sem=send_sem.at[way, zz * ny + yy, s], recv_sem=recv_sem.at[origin, s],
            device_id={"row": target(way)}, device_id_type=pl.DeviceIdType.MESH)

    def arrived(zz, yy, s, plane):
        origin = (zz * ny + yy) * nc + plane
        place = place_of(origin, s)
        pltpu.make_async_remote_copy(
            src_ref=place, dst_ref=place,
            send_sem=send_sem.at[TWIN, 0, 0], recv_sem=recv_sem.at[origin, s],
            device_id={"row": target(TWIN)}, device_id_type=pl.DeviceIdType.MESH).wait_recv()

    def maybe(way, act):
        pl.when(exists(way))(act)

    kept = pltpu.make_async_copy(own, spread.at[pl.ds(me * count, count)], own_sem.at[0])
    kept.start()
    kept_tab = pltpu.make_async_copy(own_tab, tabs.at[me], own_sem.at[1])
    kept_tab.start()

    def begin(s):
        maybe(UP, lambda: copy(UP, z, y, s, True).start())
        maybe(DOWN, lambda: copy(DOWN, z, y, s, True).start())
        copy(ACROSS, z, y, s, True).start()
        copy(TWIN, z, y, s, True).start()

    begin(TAB)
    pl.loop(0, parts)(begin)

    def along(d, s, yy, cross):
        for way, zz, there in ((UP, z - d, z >= d), (DOWN, z + d, z + d < nz)):
            @pl.when(there)
            def _(way=way, zz=zz):
                arrived(zz, yy, s, core)
                maybe(way, lambda: copy(way, zz, yy, s).start())
                if cross:
                    copy(ACROSS, zz, yy, s).start()
                copy(TWIN, zz, yy, s).start()

    other = ny - 1 - y
    arrived(z, other, 0, core)
    maybe(UP, lambda: copy(UP, z, other, 0).start())
    maybe(DOWN, lambda: copy(DOWN, z, other, 0).start())
    copy(TWIN, z, other, 0).start()

    def crossed(d, s):
        if d == 0:
            arrived(z, other, s, core)
            copy(TWIN, z, other, s).start()
        else:
            for zz, there in ((z - d, z >= d), (z + d, z + d < nz)):
                @pl.when(there)
                def _(zz=zz):
                    arrived(zz, other, s, core)
                    copy(TWIN, zz, other, s).start()

    def drain(d):
        crossed(d, TAB)
        pl.loop(1, parts)(functools.partial(crossed, d))

    for d in range(1, nz):
        along(d, 0, y, False)
        along(d, TAB, y, True)

        @pl.loop(1, parts)
        def _(s):
            along(d, s, y, True)

        along(d, 0, other, False)
        if d == 1:
            drain(0)

    for d in range(1, nz):
        drain(d)

    kept.wait()
    kept_tab.wait()

    @pl.loop(0, nz * ny)
    def _(i):
        arrived(i // ny, i % ny, TAB, nc - 1 - core)

        @pl.loop(0, parts)
        def _(s):
            arrived(i // ny, i % ny, s, nc - 1 - core)

    def sent(way, zz, yy, s):
        copy(way, zz, yy, s).wait_send()

    def finish(zz, s, first):
        for yy in range(ny):
            sent(TWIN, zz, yy, s)

        @pl.when(jnp.logical_or(jnp.logical_not(first), zz == z))
        def _():
            sent(ACROSS, zz, y, s)

        @pl.when((zz <= z) & (z + 1 < nz))
        def _():
            sent(UP, zz, y, s)

        @pl.when((zz >= z) & (z > 0))
        def _():
            sent(DOWN, zz, y, s)

        if s is not TAB:
            @pl.when(first & (zz <= z) & (z + 1 < nz))
            def _():
                sent(UP, zz, other, s)

            @pl.when(first & (zz >= z) & (z > 0))
            def _():
                sent(DOWN, zz, other, s)

    @pl.loop(0, nz)
    def _(zz):
        finish(zz, TAB, False)

        @pl.loop(0, parts)
        def _(s):
            finish(zz, s, s == 0)


def spread_all(own, own_tab, peers):
    nc, ny = 2, 2
    nz, parts = peers // (nc * ny), 8
    count, width = own.shape[0], own.shape[1]
    return pl.pallas_call(
        functools.partial(spread_kernel, nz, ny, nc, parts),
        out_shape=[
            jax.ShapeDtypeStruct((peers * count, width, width), own.dtype),
            jax.ShapeDtypeStruct((peers,) + own_tab.shape, own_tab.dtype),
        ],
        in_specs=[pl.BlockSpec(memory_space=pl.ANY)] * 2,
        out_specs=[pl.BlockSpec(memory_space=pl.ANY)] * 2,
        scratch_shapes=[
            pltpu.SemaphoreType.DMA((4, nz * ny, parts + 1)),
            pltpu.SemaphoreType.DMA((peers, parts + 1)),
            pltpu.SemaphoreType.DMA((2,)),
        ],
        compiler_params=pltpu.CompilerParams(collective_id=0, has_side_effects=True),
    )(own, own_tab)


def rebuild_kernel(terms, scale, tl, tr, tf, row, blk, tabs, whole, cot, fresh, square, right0, right1, square2, sqcot, sendback, acc, cube, both, racc, counts, parts):
    count, requests = fresh.shape[0], right0.shape[0]
    me = row[0]

    def term_ids(b):
        group, at = b // count, (b % count) * 2 * terms
        lefts = [group * count + tabs[group, 0, at + t] for t in range(terms)]
        rights = [blk[group * requests + tabs[group, 0, at + terms + t]] for t in range(terms)]
        return lefts, rights

    def product(left, lefts, rights):
        lhs = jnp.concatenate([left[i] for i in lefts], axis=1)
        rhs = jnp.concatenate([whole[i] for i in rights], axis=0)
        return scale * dot(lhs, rhs)

    @pl.loop(0, requests, unroll=4)
    def _(q):
        b = blk[me * requests + q]
        right0[q] = whole[b]
        lefts, _ = term_ids(b)
        for t, i in enumerate(lefts + [b]):
            parts[q * (terms + 1) + t] = product(whole, *term_ids(i)).astype(BF16)

    @pl.loop(0, requests, unroll=8)
    def _(q):
        _, rights = term_ids(blk[me * requests + q])
        at = q * (terms + 1)
        cubed = product(parts, [at + t for t in range(terms)], rights)
        right1[q] = (3.0 * parts[at + terms].astype(F32) - 2.0 * cubed).astype(BF16)

    square_phase(terms, scale, tl, tr, tf, whole.at[pl.ds(me * count, count)], right0, square)
    fresh_phase(terms, scale, tl, tr, tf, square, right0, fresh)
    reverse_kernel(terms, scale, tl, tr, tf, row, blk, fresh, right1, cot, square2, sqcot, sendback, acc, cube, both, racc, counts)


def call(kernel, prefetch, arrays, outs, scratch=(), flops=0, left_out=0, tight=False):
    whole = pl.BlockSpec(memory_space=pltpu.VMEM)
    smem = pl.BlockSpec(memory_space=pltpu.SMEM)
    moved = sum(a.size * a.dtype.itemsize for a in arrays)
    held = [*arrays[:len(arrays) - left_out], *outs]
    held += [s for s in scratch if getattr(s, "memory_space", None) == pltpu.VMEM]
    room = sum(math.prod(a.shape) * jnp.dtype(a.dtype).itemsize for a in held) + VMEM_SPARE
    return pl.pallas_call(
        kernel,
        out_shape=outs,
        in_specs=[smem] * len(prefetch) + [whole] * (len(arrays) - left_out) + [pl.BlockSpec(memory_space=pl.ANY)] * left_out,
        out_specs=[whole] * len(outs),
        scratch_shapes=list(scratch),
        cost_estimate=pl.CostEstimate(flops=flops, bytes_accessed=moved, transcendentals=0),
        compiler_params=pltpu.CompilerParams(vmem_limit_bytes=room if tight else VMEM_LIMIT),
    )(*prefetch, *arrays)


def body(density_guess, cotangent, term_left, term_fetch, req_owner, req_slot):
    peer_count = lax.axis_size("row")
    own_index = lax.axis_index("row")
    request_count = req_owner.shape[0] // peer_count
    slot_count = max(2, 2 * request_count // peer_count)
    blocks, width = density_guess.shape[0], density_guess.shape[1]
    terms = term_left.shape[1]
    scale = float(width * terms) ** (-0.5)
    slots = peer_count * slot_count
    row = own_index.reshape(1)
    named = req_owner[:, 0] * blocks + req_slot

    def shape(n, dtype):
        return jax.ShapeDtypeStruct((n, width, width), dtype)

    def exchange(x):
        return lax.all_to_all(x, "row", split_axis=0, concat_axis=0, tiled=True)

    work = 2 * blocks * terms * width ** 3
    common = [
        pltpu.VMEM((blocks, width, width), F32),
        pltpu.VMEM((blocks, width, width), BF16),
        pltpu.VMEM((blocks, width, 2 * width), BF16),
        pltpu.VMEM((request_count, width, width), F32),
        pltpu.SMEM((peer_count,), jnp.int32),
    ]

    landing = [pltpu.VMEM((slots, width, width), BF16), pltpu.SemaphoreType.DMA((LANDINGS,))]

    def packed(*columns):
        tab = jnp.concatenate(columns, axis=1).reshape(1, -1)
        return jnp.broadcast_to(tab, (8, tab.shape[1]))

    def routes(owner, slot):
        return owner_tables(owner, slot, own_index, peer_count, slot_count, request_count)

    if peer_count * blocks * width * width * 2 <= GATHER_BYTES and peer_count % 4 == 0:
        tab, groups = packed(term_left, term_fetch), 2
        whole, tabs = spread_all(density_guess, tab, peer_count)
        first, square1, right0, right1, square2, sqcot2, back2 = call(
            with_terms(rebuild_kernel, terms, groups, scale),
            [tab, row, named, tabs], [whole, cotangent],
            [shape(blocks, BF16), shape(blocks, BF16), shape(request_count, BF16), shape(request_count, BF16),
             shape(blocks, BF16), shape(blocks, BF16), shape(slots, BF16)],
            common + [pltpu.VMEM((request_count * (terms + 1), width, width), BF16)], flops=(peer_count + 6) * work)
        owner, slot, back2 = lax.optimization_barrier((req_owner, req_slot, back2))
        send_index, _ = routes(owner, slot)
    else:
        send_index, receive_index = routes(req_owner, req_slot)
        tab, groups = packed(term_left, term_fetch, receive_index[term_fetch]), 3
        (out0,) = call(gather_kernel, [send_index], [density_guess], [shape(slots, BF16)])
        right0 = exchange(out0)
        first, square1, out1 = call(
            with_terms(forward_kernel, terms, groups, scale), [tab, send_index], [density_guess, right0],
            [shape(blocks, BF16), shape(blocks, BF16), shape(slots, BF16)], flops=2 * work)
        right1 = exchange(out1)
        square2, sqcot2, back2 = call(
            with_terms(reverse_kernel, terms, groups, scale), [tab, row, named],
            [first, right1, cotangent],
            [shape(blocks, BF16), shape(blocks, BF16), shape(slots, BF16)], common, flops=4 * work)
    returned2 = exchange(back2)
    (second,) = call(
        with_terms(fresh_phase, terms, groups, scale), [tab], [square2, right1], [shape(blocks, BF16)], flops=work)
    local = with_terms(local_kernel, terms, groups, scale)
    (local2,) = call(local, [tab], [sqcot2, right1], [shape(blocks, F32)], flops=work)
    sqcot1, back1 = call(
        with_terms(chained_kernel, terms, groups, scale), [tab, row, named, send_index],
        [density_guess, square1, right0, local2, returned2],
        [shape(blocks, BF16), shape(slots, BF16)],
        common + [pltpu.VMEM((blocks, width, width), BF16)] + landing, flops=3 * work, left_out=1)
    returned1 = exchange(back1)
    (local1,) = call(local, [tab], [sqcot1, right0], [shape(blocks, F32)], flops=work, tight=True)
    (grad,) = call(final_kernel, [send_index], [local1, returned1], [shape(blocks, F32)], landing, left_out=1, tight=True)
    return (second, grad)


def solution(mesh):
    placed = (
        P(("groups", "row"), None, None),
        P(("groups", "row"), None, None),
        P(("groups", "row"), None),
        P(("groups", "row"), None),
        P("groups", None),
        P("groups"),
    )
    return jax.shard_map(
        body,
        mesh=mesh,
        in_specs=placed,
        out_specs=(P(("groups", "row"), None, None), P(("groups", "row"), None, None)),
        check_vma=False,
    )
```
